128 devices in a mesh: expert: 16 (over x, z), dp: 8 (over y, core).
Axes of the slice: x: 4, y: 4, z: 4, core: 2. Of those that a mesh axis runs over, the one named last changes fastest.
Arguments:
- tokens: bfloat16 [1024, 7168], P(('expert', 'dp')), may hold values from -6 to 6
- routes: int32 [1024, 8], P(('expert', 'dp')), may hold values from 0 to 15, all different within a row; in each aligned block of 64 rows (0 to 63, 64 to 127, ...) at most 48 rows name the same one
- gates: bfloat16 [1024, 8], P(('expert', 'dp')), may hold values from 0.099609375 to 1
- swapped: int32 [8], replicated, may hold values from 0 to 1, as said below
- gate_weight: bfloat16 [16, 7168, 2048], P('expert', None, 'dp'), may hold values from -6 to 6
- up_weight: bfloat16 [16, 7168, 2048], P('expert', None, 'dp'), may hold values from -6 to 6
- down_weight: bfloat16 [16, 2048, 7168], P('expert', 'dp'), may hold values from -6 to 6
Outputs:
- mixed: bfloat16 [1024, 7168], P(('expert', 'dp'))
- moved_gate: bfloat16 [16, 7168, 2048], P('expert', None, 'dp')
- moved_up: bfloat16 [16, 7168, 2048], P('expert', None, 'dp')
- moved_down: bfloat16 [16, 2048, 7168], P('expert', 'dp')
The draws below stay inside these ranges and needn't reach their ends.
Inputs may be any that keep to these rules, and one draw needn't show every extreme that they name: `routes`: each row names 8 different experts. In each aligned block of 64 rows (the tokens held by the 8 dp devices of one index along `expert` (an aligned block of 64 rows)) no expert is named by more than 48 rows, a bound that some block reaches. `swapped`: pair 0 always exchanges its slabs; each other pair does so independently with probability one half.
All inputs are finite; a program needn't handle non-finite values.
Results may differ from the reference program's by a relative error of at most 0.014.
Values may be sent and summed in bfloat16 or wider, within the bound.
A program may use at most 192 MiB of HBM per device.

```python
import math
import jax
import jax.numpy as jnp
import numpy as np
from jax import lax

D = 7168
FF = 2048
EXPERTS = 16
TOP = 8
GROUP = 64
CAP = 48
PAIRS = 8
TOKENS = 1024
N_DP = 8


def draw_swapped(key, part):
    key = jax.random.fold_in(key, 5)
    coins = jax.random.randint(key, (PAIRS,), 0, 2, dtype=jnp.int32)
    return coins.at[0].set(1).astype(jnp.int32)


def levels(own_key, shape, split, least, top_value):
    loudness, own = 1.0, jax.random.fold_in(own_key, 6)
    for dim, blocks in split:
        steps = jnp.exp(jax.random.uniform(jax.random.fold_in(own, dim), (blocks,), jnp.float32, least / len(split), top_value / len(split)))
        loudness = loudness * jnp.repeat(steps, shape[dim] // blocks).reshape([-1 if axis == dim else 1 for axis in range(len(shape))])
    return loudness


def assign_block(key, own, number, rows, number_of, top, bound, slope):
    ranking = jax.random.permutation(key, number_of)
    packed, usual = load_shares(number_of, rows * top, bound, slope, True), load_shares(number_of, rows * top, bound, slope, False)
    places = jnp.arange(number_of)

    def named(tallies, turn):
        used = int((tallies > 0).sum())
        fixed = max(1, used // 4)
        moved = fixed + (places - fixed + turn * (used - fixed)) % max(1, number_of - fixed)
        return jnp.zeros((number_of,), jnp.int32).at[ranking[jnp.where(places < fixed, places, moved)]].set(jnp.asarray(tallies, jnp.int32))

    tallies = jnp.where(number % 4 == 0, named(packed, number // 4), named(usual, number - number // 4 - 1))
    mixed = jax.random.permutation(jax.random.fold_in(own, 3), number_of)
    giver, receiver = mixed[0:number_of // 2 * 2:2], mixed[1:number_of // 2 * 2:2]
    margin = jnp.minimum(tallies[giver] - 1, bound - tallies[receiver]) // 2
    margin = jnp.where((giver == ranking[0]) | (receiver == ranking[0]) | (tallies[receiver] == 0), 0, jnp.maximum(margin, 0))
    moved = jax.random.randint(jax.random.fold_in(own, 4), (number_of // 2,), 0, 1 << 20) % (margin + 1)
    tallies = tallies.at[giver].add(-moved).at[receiver].add(moved)
    members = jnp.searchsorted(jnp.cumsum(tallies), jnp.arange(rows * top), side="right").astype(jnp.int32)
    grid = members.reshape(top, rows).T
    grid = grid[jax.random.permutation(jax.random.fold_in(own, 1), rows)]
    turn = jax.random.randint(jax.random.fold_in(own, 2), (rows, 1), 0, top)
    return jnp.take_along_axis(grid, (jnp.arange(top)[None, :] + turn) % top, axis=1)


def load_shares(amount, total, reach, skew, full):
    weights = [(1 << 20) // math.isqrt(grade ** skew) + 1 for grade in range(1, amount + 1)]
    largest = reach if full else min(reach, max(-(-total // amount), total * weights[0] // sum(weights)))
    least = 1 if total - largest >= amount - 1 else 0
    counts, surplus = [largest] + [least] * (amount - 1), total - largest - least * (amount - 1)
    while surplus > 0:
        free = [i for i in range(1, amount) if counts[i] < largest] or [i for i in range(1, amount) if counts[i] < reach]
        whole, budget = sum([weights[i] for i in free]), surplus
        for i in free:
            more = min(reach - counts[i], max(1, budget * weights[i] // whole), surplus)
            counts[i] = counts[i] + more
            surplus = surplus - more
    return np.array(counts)


def scatter_about(rng, dims, scale, limit, split=(), kind=jnp.bfloat16):
    drawn = scale * jax.random.normal(rng, dims, jnp.float32)
    if split:
        drawn = drawn * levels(rng, dims, split, -0.22, 0.18)
    return jnp.clip(drawn, -limit, limit).astype(kind)


def setup_inputs(seed: int = 0) -> dict:
    splits = jax.random.split(jax.random.key(seed), 8)
    tokens = scatter_about(splits[0], (TOKENS, D), 1.0, 6.0, ((0, 128),))
    routes_keys = jax.random.split(jax.random.fold_in(splits[1], 1), TOKENS // GROUP)
    routes_turns = jax.random.permutation(jax.random.fold_in(splits[1], 3), TOKENS // GROUP)
    routes = jax.vmap(lambda own, number: assign_block(jax.random.fold_in(splits[1], 2), own, number, GROUP, EXPERTS, TOP, CAP, 2))(routes_keys, routes_turns).reshape((TOKENS, TOP))
    gates = jnp.clip(0.099609375 + 0.9003906 * jax.random.uniform(splits[2], (TOKENS, TOP), jnp.float32) ** levels(splits[2], (TOKENS, TOP), ((0, 128),), -0.2, 0.2), 0.099609375, 1.0).astype(jnp.bfloat16)
    swapped = draw_swapped(jax.random.fold_in(splits[7], 71), 0)
    gate_weight = scatter_about(splits[4], (EXPERTS, D, FF), 1.0, 6.0, ((0, 16), (2, 8)))
    up_weight = scatter_about(splits[5], (EXPERTS, D, FF), 1.0, 6.0, ((0, 16), (2, 8)))
    down_weight = scatter_about(splits[6], (EXPERTS, FF, D), 1.0, 6.0, ((0, 16), (1, 8)))
    return {"tokens": tokens, "routes": routes, "gates": gates, "swapped": swapped, "gate_weight": gate_weight, "up_weight": up_weight, "down_weight": down_weight}


def expert_part(rows, w_gate, w_up, w_down):
    pre_gate = jnp.dot(rows, w_gate, preferred_element_type=jnp.float32) * (D ** -0.5)
    pre_up = jnp.dot(rows, w_up, preferred_element_type=jnp.float32) * (D ** -0.5)
    hidden = (jax.nn.silu(pre_gate) * pre_up).astype(jnp.bfloat16)
    return (jnp.dot(hidden, w_down, preferred_element_type=jnp.float32) * (FF ** -0.5)).astype(jnp.bfloat16)


def reference(tokens, routes, gates, swapped, gate_weight, up_weight, down_weight):
    count = EXPERTS
    half = count // 2
    slot = jnp.arange(count, dtype=jnp.int32)
    flip = jnp.concatenate([swapped, swapped])
    source = jnp.where(flip == 1, (slot + half) % count, slot).astype(jnp.int32)
    moved_gate = gate_weight[source]
    moved_up = up_weight[source]
    moved_down = down_weight[source]
    grouped = routes.reshape(count, GROUP * TOP)
    hits = (grouped[:, :, None] == slot[None, None, :]).astype(jnp.int32)
    before = jnp.cumsum(hits, axis=1) - hits
    position = jnp.sum(before * hits, axis=2).astype(jnp.int32)
    group_id = jnp.arange(count, dtype=jnp.int32)[:, None]
    entry = jnp.arange(GROUP * TOP, dtype=jnp.int32)[None, :]
    token_id = (group_id * GROUP + entry // TOP).astype(jnp.int32)
    target = ((grouped * count + group_id) * CAP + position).reshape(-1).astype(jnp.int32)
    table = jnp.full((count * count * CAP,), -1, jnp.int32).at[target].set(token_id.reshape(-1))
    scale_table = jnp.zeros((count * count * CAP,), jnp.float32).at[target].set(gates.astype(jnp.float32).reshape(-1))
    table = table.reshape(count, count * CAP)
    scale_table = scale_table.reshape(count, count * CAP)
    width = FF // N_DP

    def one_expert(total, inputs):
        ids, scales, w_gate, w_up, w_down = inputs
        safe = jnp.maximum(ids, 0).astype(jnp.int32)
        rows = jnp.where((ids >= 0)[:, None], tokens[safe], jnp.zeros((), jnp.bfloat16))
        summed = jnp.zeros((rows.shape[0], D), jnp.float32)
        for part in range(N_DP):
            low = part * width
            piece = expert_part(rows, w_gate[:, low:low + width], w_up[:, low:low + width], w_down[low:low + width])
            summed = summed + piece.astype(jnp.float32)
        return total.at[safe].add(scales[:, None] * summed), None

    total, _ = lax.scan(one_expert, jnp.zeros((TOKENS, D), jnp.float32), (table, scale_table, gate_weight, up_weight, down_weight))
    return total.astype(jnp.bfloat16), moved_gate, moved_up, moved_down
```

```python
import functools

import jax
import jax.numpy as jnp
from jax import lax
from jax.experimental import pallas as pl
from jax.experimental.pallas import tpu as pltpu
from jax.sharding import PartitionSpec as P

D = 7168
FF = 2048
EXPERTS = 16
Q = D // 4
EXT = 128
W0 = Q + EXT
BF = jnp.bfloat16
F32 = jnp.float32
MESH = pl.DeviceIdType.MESH


def moe_kernel(
    tok, gw, uw, dw,
    out, rg, ru, rd,
    x0, x1, o0, o1, wg, wu, wd,
    mine0, mine1, send0, send1, core0, core1,
    r1a, r1b, s2a, s2b, r2a, r2b, s3a, s3b, r3a, r3b,
    half_in, half_out, last_in,
    wsem, swap_s, swap_r, core_s, core_r, ag_s, ag_r, fw_s, fw_r, pc_s, pc_r, rs_s, rs_r,
):
    e = lax.axis_index("expert")
    d = lax.axis_index("dp")
    x, z = e // 4, lax.rem(e, 4)
    y, c = d // 2, lax.rem(d, 2)

    def shift(value, by):
        return lax.rem(value + by, 4)

    def device(px, pz, py, pc):
        return (px * 4 + pz, py * 2 + pc)

    other = device(x, z, y, 1 - c)
    along = {
        "x": lambda i: device(shift(x, i), z, y, c),
        "z": lambda i: device(x, shift(z, i), y, c),
        "y": lambda i: device(x, z, shift(y, i), c),
    }

    def remote(src, dst, ss, rs, dev):
        return pltpu.make_async_remote_copy(
            src_ref=src, dst_ref=dst, send_sem=ss, recv_sem=rs,
            device_id=dev, device_id_type=MESH,
        )

    loads = [
        pltpu.make_async_copy(gw.at[0], wg, wsem.at[0]),
        pltpu.make_async_copy(uw.at[0], wu, wsem.at[1]),
        pltpu.make_async_copy(dw.at[0], wd, wsem.at[2]),
    ]
    for cp in loads:
        cp.start()

    barrier = pltpu.get_barrier_semaphore()
    peers = [other] + [along[a](i) for a in "xzy" for i in (1, 2, 3)]
    for dev in peers:
        pl.semaphore_signal(barrier, inc=1, device_id=dev, device_id_type=MESH)
    pl.semaphore_wait(barrier, len(peers))

    first = remote(tok.at[1 - c], half_in, core_s.at[0], core_r.at[0], other)
    first.start()

    first.wait()
    own = tok[c]
    got = half_in[...]
    block = jnp.where(
        c == 0, jnp.concatenate([own, got], axis=0), jnp.concatenate([got, own], axis=0)
    ).astype(BF)
    rows16 = pl.ds(pl.multiple_of(x * 16, 16), 16)
    x0[y, z, rows16, 0:Q] = block[:, 0:Q]
    x0[y, z, rows16, Q:W0] = block[:, 2 * Q : 2 * Q + EXT]
    x1[y, z, rows16, :] = block[:, Q : 2 * Q]

    sent = []

    def gather(stream, stage, i, buf, view, axis):
        cp = remote(
            buf.at[view], buf.at[view], ag_s.at[stream, stage, i - 1], ag_r.at[stream, stage, i - 1],
            along[axis](i),
        )
        cp.start()
        sent.append(cp)

    def landed(stream, stage, i, buf, view):
        remote(
            buf.at[view], buf.at[view], ag_s.at[stream, stage, i - 1], ag_r.at[stream, stage, i - 1], other
        ).wait_recv()

    for i in (1, 2, 3):
        gather(0, 0, i, x0, (y, z, rows16), "x")
        gather(1, 0, i, x1, (y, z, rows16), "x")

    swaps = [
        remote(src.at[0], dst.at[0], swap_s.at[k], swap_r.at[k], along["x"](2))
        for k, (src, dst) in enumerate(((gw, rg), (uw, ru), (dw, rd)))
    ]
    for cp in swaps:
        cp.start()

    for i in (1, 2, 3):
        from16 = pl.ds(pl.multiple_of(shift(x, 4 - i) * 16, 16), 16)
        landed(0, 0, i, x0, (y, z, from16))
        landed(1, 0, i, x1, (y, z, from16))
    for i in (1, 2, 3):
        gather(0, 1, i, x0, (y, z), "z")
        gather(1, 1, i, x1, (y, z), "y")
    for i in (1, 2, 3):
        landed(0, 1, i, x0, (y, shift(z, 4 - i)))
        landed(1, 1, i, x1, (shift(y, 4 - i), z))
    every = slice(None)
    for i in (1, 2, 3):
        gather(0, 2, i, x0, (y,), "y")
        gather(1, 2, i, x1, (every, z), "z")

    forwards = []

    def forward(stream, i, view):
        src, dst = ((x0, o0), (x1, o1))[stream]
        cp = remote(src.at[view], dst.at[view], fw_s.at[stream, i], fw_r.at[stream, i], other)
        cp.start()
        forwards.append(cp)

    forward(0, 0, (y,))
    forward(1, 0, (every, z))
    for i in (1, 2, 3):
        view0, view1 = (shift(y, 4 - i),), (every, shift(z, 4 - i))
        landed(0, 2, i, x0, view0)
        forward(0, i, view0)
        landed(1, 2, i, x1, view1)
        forward(1, i, view1)
    for cp in forwards:
        cp.wait()
    for cp in sent:
        cp.wait_send()
    for cp in loads:
        cp.wait()

    lane = lax.broadcasted_iota(jnp.int32, (128, EXT), 1)
    lo = pl.multiple_of(c * 2 * Q, 2 * Q)
    hi = pl.multiple_of((1 - c) * 2 * Q, 2 * Q)

    def rows_of(ref, a, b):
        return ref[a, pl.ds(b * 2, 2)].reshape(128, ref.shape[-1])

    def turn(t, carry):
        a, b = t // 2, lax.rem(t, 2)
        full = rows_of(x0, a, b)
        parts = (
            (full[:, 0:Q], lo),
            (rows_of(x1, a, b), lo + Q),
            (rows_of(o0, a, b)[:, 0:Q], hi),
            (rows_of(o1, a, b), hi + Q),
        )
        gate = jnp.zeros((128, 256), F32)
        up = jnp.zeros((128, 256), F32)
        for part, start in parts:
            at = pl.ds(pl.multiple_of(start, Q), Q)
            gate += jnp.dot(part, wg[at, :], preferred_element_type=F32)
            up += jnp.dot(part, wu[at, :], preferred_element_type=F32)
        gate = gate * D ** (-0.5)
        up = up * D ** (-0.5)
        hidden = (gate / (1.0 + jnp.exp(-gate)) * up).astype(BF)
        weight = jnp.sum(
            jnp.where(lane == e, full[:, Q:W0].astype(F32), 0.0), axis=1, keepdims=True
        ) * FF ** (-0.5)
        for dst, start in ((send0, hi), (send1, hi + Q), (mine0, lo), (mine1, lo + Q)):
            at = pl.ds(pl.multiple_of(start, Q), Q)
            value = jnp.dot(hidden, wd[:, at], preferred_element_type=F32) * weight
            dst[a, pl.ds(b * 2, 2)] = value.astype(BF).reshape(2, 64, Q)
        return carry

    def part_copy(stream, a):
        src, dst = ((send0, core0), (send1, core1))[stream]
        return remote(src.at[a], dst.at[a], pc_s.at[stream, a], pc_r.at[stream, a], other)

    def quarter(a, carry):
        lax.fori_loop(2 * a, 2 * a + 2, turn, 0)
        part_copy(0, a).start()
        part_copy(1, a).start()
        return carry

    lax.fori_loop(0, 4, quarter, 0)

    def add_cores(a, carry):
        part_copy(0, a).wait()
        part_copy(1, a).wait()
        for own_ref, got_ref in ((mine0, core0), (mine1, core1)):
            for b in range(4):
                own_ref[a, b] = (own_ref[a, b].astype(F32) + got_ref[a, b].astype(F32)).astype(BF)
        return carry

    lax.fori_loop(0, 4, add_cores, 0)

    out_copies = []

    def scatter(stream, stage, i, src, dst, axis):
        cp = remote(src, dst, rs_s.at[stream, stage, i - 1], rs_r.at[stream, stage, i - 1], along[axis](i))
        cp.start()
        out_copies.append(cp)
        return cp

    def total(own_value, got_ref, at=()):
        value = own_value.astype(F32)
        for i in range(3):
            value += got_ref[(i,) + at].astype(F32)
        return value

    stage = []
    for i in (1, 2, 3):
        stage.append(scatter(0, 0, i, mine0.at[shift(y, i)], r1a.at[i - 1], "y"))
        stage.append(scatter(1, 0, i, mine1.at[:, shift(z, i)], r1b.at[i - 1], "z"))
    for cp in stage:
        cp.wait_recv()
    for b in range(4):
        s2a[b] = total(mine0[y, b], r1a, (b,)).astype(BF)
        s2b[b] = total(mine1[b, z], r1b, (b,)).astype(BF)
    stage = []
    for i in (1, 2, 3):
        stage.append(scatter(0, 1, i, s2a.at[shift(z, i)], r2a.at[i - 1], "z"))
        stage.append(scatter(1, 1, i, s2b.at[shift(y, i)], r2b.at[i - 1], "y"))
    for cp in stage:
        cp.wait_recv()
    s3a[...] = total(s2a[z], r2a).astype(BF)
    s3b[...] = total(s2b[y], r2b).astype(BF)
    stage = []
    for i in (1, 2, 3):
        to16 = pl.ds(pl.multiple_of(shift(x, i) * 16, 16), 16)
        stage.append(scatter(0, 2, i, s3a.at[to16], r3a.at[i - 1], "x"))
        stage.append(scatter(1, 2, i, s3b.at[to16], r3b.at[i - 1], "x"))
    for cp in stage:
        cp.wait_recv()
    sum_a = total(s3a[rows16, :], r3a)
    sum_b = total(s3b[rows16, :], r3b)
    keep_a = jnp.where(c == 0, sum_a[0:8], sum_a[8:16])
    keep_b = jnp.where(c == 0, sum_b[0:8], sum_b[8:16])
    half_out[:, 0:Q] = jnp.where(c == 0, sum_a[8:16], sum_a[0:8])
    half_out[:, Q : 2 * Q] = jnp.where(c == 0, sum_b[8:16], sum_b[0:8])
    last = remote(half_out, last_in, core_s.at[1], core_r.at[1], other)
    last.start()
    last.wait()
    kept = jnp.concatenate([keep_a, keep_b], axis=1)
    given = last_in[...]
    out[:, 0 : 2 * Q] = jnp.where(c == 0, kept, given).astype(BF)
    out[:, 2 * Q :] = jnp.where(c == 0, given, kept).astype(BF)

    for cp in out_copies:
        cp.wait_send()
    for cp in swaps:
        cp.wait()


def moe(tok, gate_weight, up_weight, down_weight):
    vm = lambda *shape: pltpu.VMEM(shape, BF)
    dma = lambda *shape: pltpu.SemaphoreType.DMA(shape)
    any_spec = pl.BlockSpec(memory_space=pl.ANY)
    vmem_spec = pl.BlockSpec(memory_space=pltpu.VMEM)
    like = lambda a: jax.ShapeDtypeStruct(a.shape, a.dtype)
    return pl.pallas_call(
        moe_kernel,
        out_shape=(
            jax.ShapeDtypeStruct((8, D), BF),
            like(gate_weight), like(up_weight), like(down_weight),
        ),
        in_specs=[vmem_spec, any_spec, any_spec, any_spec],
        out_specs=(vmem_spec, any_spec, any_spec, any_spec),
        scratch_shapes=[
            vm(4, 4, 64, W0), vm(4, 4, 64, Q), vm(4, 4, 64, W0), vm(4, 4, 64, Q),
            vm(D, 256), vm(D, 256), vm(256, D),
            vm(4, 4, 64, Q), vm(4, 4, 64, Q), vm(4, 4, 64, Q), vm(4, 4, 64, Q),
            vm(4, 4, 64, Q), vm(4, 4, 64, Q),
            vm(3, 4, 64, Q), vm(3, 4, 64, Q), vm(4, 64, Q), vm(4, 64, Q),
            vm(3, 64, Q), vm(3, 64, Q), vm(64, Q), vm(64, Q), vm(3, 16, Q), vm(3, 16, Q),
            pltpu.VMEM((8, 2 * Q + EXT), F32), pltpu.VMEM((8, 2 * Q), F32), pltpu.VMEM((8, 2 * Q), F32),
            dma(3), dma(3), dma(3), dma(2), dma(2),
            dma(2, 3, 3), dma(2, 3, 3), dma(2, 4), dma(2, 4), dma(2, 4), dma(2, 4),
            dma(2, 3, 3), dma(2, 3, 3),
        ],
        compiler_params=pltpu.CompilerParams(
            collective_id=0, has_side_effects=True, vmem_limit_bytes=64 * 1024 * 1024
        ),
        cost_estimate=pl.CostEstimate(
            flops=6 * 1024 * D * 256, bytes_accessed=33 * 1024 * 1024, transcendentals=1024 * 256
        ),
        name="moe_and_exchange",
    )(tok, gate_weight, up_weight, down_weight)


PIECES = 8


def pick_kernel(flag, og, ou, od, rg, ru, rd, mg, mu, md, bg, bu, bd, in_sem, out_sem):
    outs, bufs = (mg, mu, md), (bg, bu, bd)

    def go(sources):
        loads, stores = [], []
        for part in range(PIECES):
            for k, (src, buf, dst) in enumerate(zip(sources, bufs, outs)):
                rows = src.shape[1] // PIECES
                at = pl.ds(part * rows, rows)
                loads.append(pltpu.make_async_copy(src.at[0, at], buf.at[at], in_sem.at[k, part]))
                stores.append(pltpu.make_async_copy(buf.at[at], dst.at[0, at], out_sem.at[k, part]))
        for cp in loads:
            cp.start()
        for load, store in zip(loads, stores):
            load.wait()
            store.start()
        for cp in stores:
            cp.wait()

    @pl.when(flag[0] == 1)
    def _():
        go((rg, ru, rd))

    @pl.when(flag[0] != 1)
    def _():
        go((og, ou, od))


def pick(flag, own, received):
    any_spec = pl.BlockSpec(memory_space=pl.ANY)
    return pl.pallas_call(
        pick_kernel,
        out_shape=tuple(jax.ShapeDtypeStruct(a.shape, a.dtype) for a in own),
        in_specs=[pl.BlockSpec(memory_space=pltpu.SMEM)] + [any_spec] * 6,
        out_specs=(any_spec,) * 3,
        scratch_shapes=[pltpu.VMEM(a.shape[1:], a.dtype) for a in own]
        + [pltpu.SemaphoreType.DMA((3, PIECES)), pltpu.SemaphoreType.DMA((3, PIECES))],
        compiler_params=pltpu.CompilerParams(vmem_limit_bytes=64 * 1024 * 1024),
        name="pick_slab",
    )(flag, *own, *received)


def on_device(tokens, routes, gates, swapped, gate_weight, up_weight, down_weight):
    mine = lax.axis_index("expert")
    named = routes[:, :, None] == jnp.arange(EXT, dtype=jnp.int32)
    by_expert = jnp.sum(jnp.where(named, gates.astype(F32)[:, :, None], 0.0), axis=1)
    wide = tokens.astype(F32)
    tok = jnp.stack(
        [jnp.concatenate([wide[:, k * 2 * Q : (k + 1) * 2 * Q], by_expert], axis=1) for k in (0, 1)]
    )
    mixed, *received = moe(tok, gate_weight, up_weight, down_weight)
    flag = lax.dynamic_slice(swapped, (lax.rem(mine, EXPERTS // 2),), (1,))
    moved = pick(flag, (gate_weight, up_weight, down_weight), received)
    return (mixed, *moved)


def solution(mesh):
    in_specs = (
        P(("expert", "dp"), None),
        P(("expert", "dp"), None),
        P(("expert", "dp"), None),
        P(),
        P("expert", None, "dp"),
        P("expert", None, "dp"),
        P("expert", "dp", None),
    )
    out_specs = (
        P(("expert", "dp"), None),
        P("expert", None, "dp"),
        P("expert", None, "dp"),
        P("expert", "dp", None),
    )
    return jax.shard_map(
        on_device, mesh=mesh, in_specs=in_specs, out_specs=out_specs, check_vma=False
    )
```

```python
import functools

import jax
import jax.numpy as jnp
from jax import lax
from jax.experimental import pallas as pl
from jax.experimental.pallas import tpu as pltpu
from jax.sharding import PartitionSpec as P

D = 7168
FF = 2048
EXPERTS = 16
Q = D // 4
EXT = 128
W0 = Q + EXT
BF = jnp.bfloat16
F32 = jnp.float32
MESH = pl.DeviceIdType.MESH
PIECES = 8
FIRST, SECOND, THIRD, FOURTH = 1, 14, 2, 2


def moe_kernel(
    tok, routes, gates, gw, uw, dw,
    out, rg, ru, rd,
    x0, x1, o0, o1, wg, wu, wd,
    mine0, mine1, send0, send1, core0, core1,
    r1a, r1b, s2a, s2b, r2a, r2b, s3a, s3b, r3a, r3b,
    half_to, half_in, half_out, last_in,
    wsem, swap_s, swap_r, core_s, core_r, ag_s, ag_r, fw_s, fw_r, pc_s, pc_r, rs_s, rs_r,
):
    e = lax.axis_index("expert")
    d = lax.axis_index("dp")
    x, z = e // 4, lax.rem(e, 4)
    y, c = d // 2, lax.rem(d, 2)

    def shift(value, by):
        return lax.rem(value + by, 4)

    def device(px, pz, py, pc):
        return (px * 4 + pz, py * 2 + pc)

    other = device(x, z, y, 1 - c)
    along = {
        "x": lambda i: device(shift(x, i), z, y, c),
        "z": lambda i: device(x, shift(z, i), y, c),
        "y": lambda i: device(x, z, shift(y, i), c),
    }

    def remote(src, dst, ss, rs, dev):
        return pltpu.make_async_remote_copy(
            src_ref=src, dst_ref=dst, send_sem=ss, recv_sem=rs,
            device_id=dev, device_id_type=MESH,
        )

    loads = [
        pltpu.make_async_copy(gw.at[0], wg, wsem.at[0]),
        pltpu.make_async_copy(uw.at[0], wu, wsem.at[1]),
        pltpu.make_async_copy(dw.at[0], wd, wsem.at[2]),
    ]
    for cp in loads:
        cp.start()

    barrier = pltpu.get_barrier_semaphore()
    peers = [other] + [along[a](i) for a in "xzy" for i in (1, 2, 3)]
    for dev in peers:
        pl.semaphore_signal(barrier, inc=1, device_id=dev, device_id_type=MESH)

    wide = tok[...].astype(F32)
    named, level = routes[...], gates[...].astype(F32)
    slot = lax.broadcasted_iota(jnp.int32, (8, EXT), 1)
    by_expert = jnp.zeros((8, EXT), F32)
    for k in range(8):
        by_expert += jnp.where(named[:, k : k + 1] == slot, level[:, k : k + 1], 0.0)
    low, high = wide[:, 0 : 2 * Q], wide[:, 2 * Q :]
    half_to[:, 0 : 2 * Q] = jnp.where(c == 0, high, low)
    half_to[:, 2 * Q :] = by_expert
    own = jnp.concatenate([jnp.where(c == 0, low, high), by_expert], axis=1)
    pl.semaphore_wait(barrier, len(peers))

    def slab_piece(k, part):
        src, dst = ((gw, rg), (uw, ru), (dw, rd))[k]
        rows = src.shape[1] // PIECES
        at = (0, pl.ds(part * rows, rows))
        return remote(src.at[at], dst.at[at], swap_s.at[k, part], swap_r.at[k, part], along["x"](2))

    swaps = [slab_piece(k, part) for k in range(3) for part in range(PIECES)]
    waiting = list(swaps)

    def send_pieces(number):
        for cp in waiting[:number]:
            cp.start()
        del waiting[:number]

    send_pieces(FIRST)

    first = remote(half_to, half_in, core_s.at[0], core_r.at[0], other)
    first.start()

    first.wait()
    got = half_in[...]
    block = jnp.where(
        c == 0, jnp.concatenate([own, got], axis=0), jnp.concatenate([got, own], axis=0)
    ).astype(BF)
    rows16 = pl.ds(pl.multiple_of(x * 16, 16), 16)
    x0[y, z, rows16, 0:Q] = block[:, 0:Q]
    x0[y, z, rows16, Q:W0] = block[:, 2 * Q : 2 * Q + EXT]
    x1[y, z, rows16, :] = block[:, Q : 2 * Q]

    sent = []

    def gather(stream, stage, i, buf, view, axis):
        cp = remote(
            buf.at[view], buf.at[view], ag_s.at[stream, stage, i - 1], ag_r.at[stream, stage, i - 1],
            along[axis](i),
        )
        cp.start()
        sent.append(cp)

    def landed(stream, stage, i, buf, view):
        remote(
            buf.at[view], buf.at[view], ag_s.at[stream, stage, i - 1], ag_r.at[stream, stage, i - 1], other
        ).wait_recv()

    for i in (1, 2, 3):
        gather(0, 0, i, x0, (y, z, rows16), "x")
        gather(1, 0, i, x1, (y, z, rows16), "x")
    send_pieces(SECOND)

    for i in (1, 2, 3):
        from16 = pl.ds(pl.multiple_of(shift(x, 4 - i) * 16, 16), 16)
        landed(0, 0, i, x0, (y, z, from16))
        landed(1, 0, i, x1, (y, z, from16))
    for i in (1, 2, 3):
        gather(0, 1, i, x0, (y, z), "z")
        gather(1, 1, i, x1, (y, z), "y")
    for i in (1, 2, 3):
        landed(0, 1, i, x0, (y, shift(z, 4 - i)))
        landed(1, 1, i, x1, (shift(y, 4 - i), z))
    every = slice(None)
    for i in (1, 2, 3):
        gather(0, 2, i, x0, (y,), "y")
        gather(1, 2, i, x1, (every, z), "z")

    forwards = []

    def forward(stream, i, view):
        src, dst = ((x0, o0), (x1, o1))[stream]
        cp = remote(src.at[view], dst.at[view], fw_s.at[stream, i], fw_r.at[stream, i], other)
        cp.start()
        forwards.append(cp)

    forward(0, 0, (y,))
    forward(1, 0, (every, z))
    for i in (1, 2, 3):
        view0, view1 = (shift(y, 4 - i),), (every, shift(z, 4 - i))
        landed(0, 2, i, x0, view0)
        forward(0, i, view0)
        landed(1, 2, i, x1, view1)
        forward(1, i, view1)
    for cp in forwards:
        cp.wait()
    for cp in sent:
        cp.wait_send()
    for cp in loads:
        cp.wait()

    lane = lax.broadcasted_iota(jnp.int32, (128, EXT), 1)
    lo = pl.multiple_of(c * 2 * Q, 2 * Q)
    hi = pl.multiple_of((1 - c) * 2 * Q, 2 * Q)

    def rows_of(ref, a, b):
        return ref[a, pl.ds(b * 2, 2)].reshape(128, ref.shape[-1])

    def turn(t, carry):
        a, b = t // 2, lax.rem(t, 2)
        full = rows_of(x0, a, b)
        parts = (
            (full[:, 0:Q], lo),
            (rows_of(x1, a, b), lo + Q),
            (rows_of(o0, a, b)[:, 0:Q], hi),
            (rows_of(o1, a, b), hi + Q),
        )
        gate = jnp.zeros((128, 256), F32)
        up = jnp.zeros((128, 256), F32)
        for part, start in parts:
            at = pl.ds(pl.multiple_of(start, Q), Q)
            gate += jnp.dot(part, wg[at, :], preferred_element_type=F32)
            up += jnp.dot(part, wu[at, :], preferred_element_type=F32)
        gate = gate * D ** (-0.5)
        up = up * D ** (-0.5)
        hidden = (gate / (1.0 + jnp.exp(-gate)) * up).astype(BF)
        weight = jnp.sum(
            jnp.where(lane == e, full[:, Q:W0].astype(F32), 0.0), axis=1, keepdims=True
        ) * FF ** (-0.5)
        for dst, start in ((send0, hi), (send1, hi + Q), (mine0, lo), (mine1, lo + Q)):
            at = pl.ds(pl.multiple_of(start, Q), Q)
            value = jnp.dot(hidden, wd[:, at], preferred_element_type=F32) * weight
            dst[a, pl.ds(b * 2, 2)] = value.astype(BF).reshape(2, 64, Q)
        return carry

    def part_copy(stream, a):
        src, dst = ((send0, core0), (send1, core1))[stream]
        return remote(src.at[a], dst.at[a], pc_s.at[stream, a], pc_r.at[stream, a], other)

    def quarter(a, carry):
        lax.fori_loop(2 * a, 2 * a + 2, turn, 0)
        part_copy(0, a).start()
        part_copy(1, a).start()
        return carry

    lax.fori_loop(0, 4, quarter, 0)

    send_pieces(THIRD)

    def add_cores(a, carry):
        part_copy(0, a).wait()
        part_copy(1, a).wait()
        for own_ref, got_ref in ((mine0, core0), (mine1, core1)):
            for b in range(4):
                own_ref[a, b] = (own_ref[a, b].astype(F32) + got_ref[a, b].astype(F32)).astype(BF)
        return carry

    lax.fori_loop(0, 4, add_cores, 0)

    out_copies = []

    def scatter(stream, stage, i, src, dst, axis):
        cp = remote(src, dst, rs_s.at[stream, stage, i - 1], rs_r.at[stream, stage, i - 1], along[axis](i))
        cp.start()
        out_copies.append(cp)
        return cp

    def total(own_value, got_ref, at=()):
        value = own_value.astype(F32)
        for i in range(3):
            value += got_ref[(i,) + at].astype(F32)
        return value

    stage = []
    for i in (1, 2, 3):
        stage.append(scatter(0, 0, i, mine0.at[shift(y, i)], r1a.at[i - 1], "y"))
        stage.append(scatter(1, 0, i, mine1.at[:, shift(z, i)], r1b.at[i - 1], "z"))
    for cp in stage:
        cp.wait_recv()
    for b in range(4):
        s2a[b] = total(mine0[y, b], r1a, (b,)).astype(BF)
        s2b[b] = total(mine1[b, z], r1b, (b,)).astype(BF)
    stage = []
    for i in (1, 2, 3):
        stage.append(scatter(0, 1, i, s2a.at[shift(z, i)], r2a.at[i - 1], "z"))
        stage.append(scatter(1, 1, i, s2b.at[shift(y, i)], r2b.at[i - 1], "y"))
    send_pieces(FOURTH)
    for cp in stage:
        cp.wait_recv()
    s3a[...] = total(s2a[z], r2a).astype(BF)
    s3b[...] = total(s2b[y], r2b).astype(BF)
    stage = []
    for i in (1, 2, 3):
        to16 = pl.ds(pl.multiple_of(shift(x, i) * 16, 16), 16)
        stage.append(scatter(0, 2, i, s3a.at[to16], r3a.at[i - 1], "x"))
        stage.append(scatter(1, 2, i, s3b.at[to16], r3b.at[i - 1], "x"))
    send_pieces(len(waiting))
    for cp in stage:
        cp.wait_recv()
    sum_a = total(s3a[rows16, :], r3a)
    sum_b = total(s3b[rows16, :], r3b)
    keep_a = jnp.where(c == 0, sum_a[0:8], sum_a[8:16])
    keep_b = jnp.where(c == 0, sum_b[0:8], sum_b[8:16])
    half_out[:, 0:Q] = jnp.where(c == 0, sum_a[8:16], sum_a[0:8])
    half_out[:, Q : 2 * Q] = jnp.where(c == 0, sum_b[8:16], sum_b[0:8])
    last = remote(half_out, last_in, core_s.at[1], core_r.at[1], other)
    last.start()
    last.wait()
    kept = jnp.concatenate([keep_a, keep_b], axis=1)
    given = last_in[...]
    out[:, 0 : 2 * Q] = jnp.where(c == 0, kept, given).astype(BF)
    out[:, 2 * Q :] = jnp.where(c == 0, given, kept).astype(BF)

    for cp in out_copies:
        cp.wait_send()
    for cp in swaps:
        cp.wait()


def moe(tok, routes, gates, gate_weight, up_weight, down_weight):
    vm = lambda *shape: pltpu.VMEM(shape, BF)
    dma = lambda *shape: pltpu.SemaphoreType.DMA(shape)
    any_spec = pl.BlockSpec(memory_space=pl.ANY)
    vmem_spec = pl.BlockSpec(memory_space=pltpu.VMEM)
    like = lambda a: jax.ShapeDtypeStruct(a.shape, a.dtype)
    return pl.pallas_call(
        moe_kernel,
        out_shape=(
            jax.ShapeDtypeStruct((8, D), BF),
            like(gate_weight), like(up_weight), like(down_weight),
        ),
        in_specs=[vmem_spec] * 3 + [any_spec] * 3,
        out_specs=(vmem_spec, any_spec, any_spec, any_spec),
        scratch_shapes=[
            vm(4, 4, 64, W0), vm(4, 4, 64, Q), vm(4, 4, 64, W0), vm(4, 4, 64, Q),
            vm(D, 256), vm(D, 256), vm(256, D),
            vm(4, 4, 64, Q), vm(4, 4, 64, Q), vm(4, 4, 64, Q), vm(4, 4, 64, Q),
            vm(4, 4, 64, Q), vm(4, 4, 64, Q),
            vm(3, 4, 64, Q), vm(3, 4, 64, Q), vm(4, 64, Q), vm(4, 64, Q),
            vm(3, 64, Q), vm(3, 64, Q), vm(64, Q), vm(64, Q), vm(3, 16, Q), vm(3, 16, Q),
            pltpu.VMEM((8, 2 * Q + EXT), F32), pltpu.VMEM((8, 2 * Q + EXT), F32),
            pltpu.VMEM((8, 2 * Q), F32), pltpu.VMEM((8, 2 * Q), F32),
            dma(3), dma(3, PIECES), dma(3, PIECES), dma(2), dma(2),
            dma(2, 3, 3), dma(2, 3, 3), dma(2, 4), dma(2, 4), dma(2, 4), dma(2, 4),
            dma(2, 3, 3), dma(2, 3, 3),
        ],
        compiler_params=pltpu.CompilerParams(
            collective_id=0, has_side_effects=True, vmem_limit_bytes=64 * 1024 * 1024
        ),
        cost_estimate=pl.CostEstimate(
            flops=6 * 1024 * D * 256, bytes_accessed=33 * 1024 * 1024, transcendentals=1024 * 256
        ),
        name="moe_and_exchange",
    )(tok, routes, gates, gate_weight, up_weight, down_weight)


def pick_kernel(swapped, og, ou, od, rg, ru, rd, mg, mu, md, bg, bu, bd, in_sem, out_sem):
    outs, bufs = (mg, mu, md), (bg, bu, bd)
    flag = swapped[lax.rem(lax.axis_index("expert"), EXPERTS // 2)]

    def go(sources):
        loads, stores = [], []
        for part in range(PIECES):
            for k, (src, buf, dst) in enumerate(zip(sources, bufs, outs)):
                rows = src.shape[1] // PIECES
                at = pl.ds(part * rows, rows)
                loads.append(pltpu.make_async_copy(src.at[0, at], buf.at[at], in_sem.at[k, part]))
                stores.append(pltpu.make_async_copy(buf.at[at], dst.at[0, at], out_sem.at[k, part]))
        for cp in loads:
            cp.start()
        for load, store in zip(loads, stores):
            load.wait()
            store.start()
        for cp in stores:
            cp.wait()

    @pl.when(flag == 1)
    def _():
        go((rg, ru, rd))

    @pl.when(flag != 1)
    def _():
        go((og, ou, od))


def pick(swapped, own, received):
    any_spec = pl.BlockSpec(memory_space=pl.ANY)
    return pl.pallas_call(
        pick_kernel,
        out_shape=tuple(jax.ShapeDtypeStruct(a.shape, a.dtype) for a in own),
        in_specs=[pl.BlockSpec(memory_space=pltpu.SMEM)] + [any_spec] * 6,
        out_specs=(any_spec,) * 3,
        scratch_shapes=[pltpu.VMEM(a.shape[1:], a.dtype) for a in own]
        + [pltpu.SemaphoreType.DMA((3, PIECES)), pltpu.SemaphoreType.DMA((3, PIECES))],
        compiler_params=pltpu.CompilerParams(vmem_limit_bytes=64 * 1024 * 1024),
        name="pick_slab",
    )(swapped, *own, *received)


def on_device(tokens, routes, gates, swapped, gate_weight, up_weight, down_weight):
    mixed, *received = moe(tokens, routes, gates, gate_weight, up_weight, down_weight)
    moved = pick(swapped, (gate_weight, up_weight, down_weight), received)
    return (mixed, *moved)


def solution(mesh):
    in_specs = (
        P(("expert", "dp"), None),
        P(("expert", "dp"), None),
        P(("expert", "dp"), None),
        P(),
        P("expert", None, "dp"),
        P("expert", None, "dp"),
        P("expert", "dp", None),
    )
    out_specs = (
        P(("expert", "dp"), None),
        P("expert", None, "dp"),
        P("expert", None, "dp"),
        P("expert", "dp", None),
    )
    return jax.shard_map(
        on_device, mesh=mesh, in_specs=in_specs, out_specs=out_specs, check_vma=False
    )
```

```python
import functools

import jax
import jax.numpy as jnp
from jax import lax
from jax.experimental import pallas as pl
from jax.experimental.pallas import tpu as pltpu
from jax.sharding import PartitionSpec as P

D = 7168
FF = 2048
EXPERTS = 16
Q = D // 4
EXT = 128
W0 = Q + EXT
BF = jnp.bfloat16
F32 = jnp.float32
MESH = pl.DeviceIdType.MESH
PIECES = 8
FIRST, SECOND, THIRD, FOURTH = 1, 11, 2, 1

CHUNKS = 8
UNIT = 16

ROUTES = {
    15: ((1, 29), (0, 27), (11, 29), (10, 27), (21, 29), (20, 27), (31, 29), (30, 27)),
    41: ((1, 22), (0, 20), (3, 7), (5, 7), (29, 13), (31, 23), (30, 20), (43, 23), (42, 13), (45, 20)),
    51: ((1, 29), (7, 27), (11, 29), (13, 27), (33, 29), (39, 27), (43, 29), (45, 27)),
    61: ((1, 36), (3, 20), (19, 13), (21, 36), (20, 7), (31, 36), (30, 20), (33, 36), (37, 7), (39, 13), (43, 36), (45, 20)),
    85: ((1, 29), (3, 27), (21, 29), (23, 27), (33, 29), (35, 27), (53, 29), (55, 27)),
    103: ((1, 36), (0, 20), (8, 6), (11, 37), (15, 13), (21, 36), (23, 20), (41, 6), (43, 37), (47, 13), (53, 36), (55, 20)),
    107: ((1, 36), (0, 20), (11, 36), (13, 20), (29, 13), (31, 36), (30, 7), (41, 13), (43, 36), (47, 7), (53, 36), (55, 20)),
    119: ((1, 43), (7, 13), (11, 43), (15, 13), (21, 43), (23, 13), (33, 43), (39, 13), (43, 43), (47, 13), (53, 43), (55, 13)),
    127: ((1, 50), (6, 6), (11, 50), (14, 6), (21, 50), (22, 6), (31, 50), (30, 6), (33, 50), (39, 6), (43, 50), (47, 6), (53, 50), (55, 6)),
    151: ((1, 36), (7, 20), (11, 36), (10, 20), (21, 36), (20, 20), (33, 36), (35, 13), (37, 7), (61, 7), (63, 36), (62, 13)),
    153: ((1, 29), (3, 27), (29, 27), (31, 29), (33, 29), (35, 27), (61, 27), (63, 29)),
    165: ((1, 29), (3, 27), (21, 29), (23, 27), (43, 29), (45, 27), (57, 27), (63, 29)),
    171: ((1, 36), (0, 20), (8, 6), (11, 37), (13, 13), (29, 20), (31, 36), (41, 6), (43, 37), (45, 13), (61, 20), (63, 36)),
    187: ((1, 43), (5, 13), (11, 43), (13, 13), (29, 13), (31, 43), (33, 43), (37, 13), (43, 43), (45, 13), (61, 13), (63, 43)),
    195: ((1, 29), (0, 27), (11, 29), (13, 27), (51, 27), (53, 29), (63, 29), (62, 27)),
    205: ((1, 36), (0, 20), (19, 20), (21, 36), (24, 6), (27, 13), (31, 37), (51, 20), (53, 36), (57, 6), (59, 13), (63, 37)),
    219: ((1, 43), (5, 13), (11, 43), (10, 13), (29, 13), (31, 43), (33, 43), (35, 13), (53, 43), (52, 13), (59, 13), (63, 43)),
    221: ((1, 43), (3, 13), (19, 13), (21, 43), (27, 13), (31, 43), (33, 43), (35, 13), (51, 13), (53, 43), (59, 13), (63, 43)),
    231: ((1, 43), (7, 13), (11, 43), (15, 13), (21, 43), (23, 13), (41, 13), (43, 43), (49, 13), (53, 43), (57, 13), (63, 43)),
    237: ((1, 43), (3, 13), (19, 13), (21, 43), (27, 13), (31, 43), (41, 13), (43, 43), (49, 13), (53, 43), (57, 13), (63, 43)),
    239: ((1, 50), (0, 6), (8, 6), (11, 50), (16, 6), (21, 50), (24, 6), (31, 50), (41, 6), (43, 50), (49, 6), (53, 50), (57, 6), (63, 50)),
    241: ((1, 36), (3, 6), (7, 14), (33, 37), (34, 7), (36, 12), (43, 36), (42, 20), (53, 36), (52, 20), (63, 36), (62, 20)),
    247: ((1, 50), (7, 6), (11, 50), (15, 6), (21, 50), (23, 6), (33, 50), (38, 6), (43, 50), (46, 6), (53, 50), (54, 6), (63, 50), (62, 6)),
    255: ((1, 56), (11, 56), (21, 56), (31, 56), (33, 56), (43, 56), (53, 56), (63, 56)),
}
SETS = sorted(ROUTES)
SERVES = (
    1, 0, 0, 0, 1, 0, 0, 0, 2, 2, 4, 9, 10, 13, 3, 8,
    1, 2, 11, 5, 1, 12, 3, 8, 2, 2, 3, 7, 3, 13, 3, 8,
    4, 14, 4, 5, 15, 6, 15, 8, 4, 7, 4, 7, 16, 16, 17, 8,
    5, 5, 5, 5, 6, 6, 19, 8, 21, 7, 7, 7, 8, 8, 8, 8,
    10, 14, 11, 9, 10, 12, 15, 20, 10, 9, 9, 9, 10, 13, 17, 23,
    11, 12, 11, 18, 12, 12, 19, 20, 21, 13, 22, 22, 13, 13, 23, 23,
    14, 14, 15, 18, 15, 16, 15, 20, 21, 16, 17, 22, 16, 16, 17, 23,
    21, 18, 18, 18, 19, 20, 19, 20, 21, 22, 22, 22, 23, 23, 23, 23,
)


def legs_of(z, ring, direct, sign):
    stops = [(0, z)]
    if ring != z:
        stops.append((0, ring))
    if not direct:
        stops.append((-sign, ring))
    stops.append((2, z))
    return list(zip(stops[:-1], stops[1:]))


class Leg:
    pass


def layout(pairs):
    lands, relay_rows = {}, {}
    legs = []
    base = {}
    for code, units in ROUTES[pairs]:
        parity, z, ring, direct = code // 32, code // 8 % 4, code // 2 % 4, code % 2
        rows = units * UNIT
        start = base.get((parity, z), 0)
        base[parity, z] = start + rows * CHUNKS
        before = None
        steps = legs_of(z, ring, direct, 1 - 2 * parity)
        for k, (a, b) in enumerate(steps):
            leg = Leg()
            leg.rows, leg.start, leg.before, leg.turn = rows, start, before, k
            leg.final = k == len(steps) - 1
            leg.move = (b[0] - a[0], b[1])
            leg.back = (a[0] - b[0], a[1])
            leg.sender = ((parity + a[0]) % 2, a[1])
            leg.taker = ((parity + b[0]) % 2, b[1])
            if not leg.final:
                leg.land_slot = lands.get(leg.taker, 0)
                lands[leg.taker] = leg.land_slot + 1
                leg.relay = relay_rows.get(leg.taker, 0)
                relay_rows[leg.taker] = leg.relay + rows * CHUNKS
            legs.append(leg)
            before = leg
    return legs, max(lands.values(), default=1), max(relay_rows.values(), default=UNIT)


def exchange_kernel(legs, src, dst, relay, end_sem, land_sem):
    e = lax.axis_index("expert")
    d = lax.axis_index("dp")
    x, z = e // 4, lax.rem(e, 4)

    def device(move):
        return (lax.rem(x + move[0] + 4, 4) * 4 + move[1], d)

    kinds = sorted({leg.sender for leg in legs} | {leg.taker for leg in legs})
    barrier = pltpu.get_barrier_semaphore()
    for kind in kinds:
        @pl.when((lax.rem(x, 2) == kind[0]) & (z == kind[1]))
        def _(kind=kind):
            peers = {(leg.move[0] % 4, leg.move[1]) for leg in legs if leg.sender == kind}
            peers |= {(leg.back[0] % 4, leg.back[1]) for leg in legs if leg.taker == kind}
            for move in sorted(peers):
                pl.semaphore_signal(barrier, inc=1, device_id=device(move), device_id_type=MESH)
            pl.semaphore_wait(barrier, len(peers))

    def own(leg, chunk):
        return pl.ds(pl.multiple_of(leg.start + chunk * leg.rows, UNIT), leg.rows)

    def spot(leg, chunk):
        if leg.final:
            return dst.at[0, own(leg, chunk)]
        return relay.at[pl.ds(pl.multiple_of(leg.relay + chunk * leg.rows, UNIT), leg.rows)]

    def copy(leg, chunk):
        return pltpu.make_async_remote_copy(
            src_ref=src.at[0, own(leg, chunk)] if leg.turn == 0 else spot(leg.before, chunk),
            dst_ref=spot(leg, chunk),
            send_sem=end_sem.at[min(leg.turn, 1)],
            recv_sem=end_sem.at[2] if leg.final else land_sem.at[leg.land_slot, chunk],
            device_id=device(leg.move), device_id_type=MESH,
        )

    def arrival(leg, chunk):
        here = spot(leg, chunk)
        return pltpu.make_async_remote_copy(
            src_ref=here, dst_ref=here,
            send_sem=end_sem.at[0],
            recv_sem=land_sem.at[leg.land_slot, chunk],
            device_id=device((2, z)), device_id_type=MESH,
        )

    def whole(ref):
        return pltpu.make_async_remote_copy(
            src_ref=ref, dst_ref=ref, send_sem=end_sem.at[0], recv_sem=end_sem.at[2],
            device_id=device((2, z)), device_id_type=MESH,
        )

    for kind in kinds:
        @pl.when((lax.rem(x, 2) == kind[0]) & (z == kind[1]))
        def _(kind=kind):
            out = [leg for leg in legs if leg.sender == kind]
            late = max([leg.turn for leg in out], default=0)

            def push(step, carry):
                for turn in range(late + 1):
                    chunk = step - turn

                    @pl.when((chunk >= 0) & (chunk < CHUNKS))
                    def _(turn=turn, chunk=chunk):
                        for leg in out:
                            if leg.turn == turn:
                                if turn:
                                    arrival(leg.before, chunk).wait_recv()
                                copy(leg, chunk).start()
                return carry

            if out:
                lax.fori_loop(0, CHUNKS + late, push, 0)
            passed = sum(leg.rows for leg in out if leg.turn) * CHUNKS
            if any(leg.final and leg.taker == kind for leg in legs):
                whole(dst.at[0]).wait_recv()
                whole(src.at[0]).wait_send()
            if passed:
                relayed = relay.at[pl.ds(0, passed)]
                pltpu.make_async_remote_copy(
                    src_ref=relayed, dst_ref=relayed,
                    send_sem=end_sem.at[1], recv_sem=end_sem.at[2],
                    device_id=device((2, z)), device_id_type=MESH,
                ).wait_send()


def exchange(pairs, weight):
    any_spec = pl.BlockSpec(memory_space=pl.ANY)
    legs, n_land, n_relay = layout(pairs)
    return pl.pallas_call(
        functools.partial(exchange_kernel, legs),
        out_shape=jax.ShapeDtypeStruct(weight.shape, weight.dtype),
        in_specs=[any_spec],
        out_specs=any_spec,
        scratch_shapes=[
            pltpu.VMEM((n_relay, 256), BF),
            pltpu.SemaphoreType.DMA((3,)),
            pltpu.SemaphoreType.DMA((n_land, CHUNKS)),
        ],
        compiler_params=pltpu.CompilerParams(
            collective_id=1 + pairs // 2, has_side_effects=True, vmem_limit_bytes=60 * 1024 * 1024
        ),
        cost_estimate=pl.CostEstimate(flops=0, bytes_accessed=64 * 1024 * 1024, transcendentals=0),
        name="exchange_%d" % pairs,
    )(weight)


def moe_kernel(
    tok, routes, gates, gw, uw, dw,
    out, rg, rd,
    x0, x1, o0, o1, wg, wu, wd,
    mine0, mine1, send0, send1, core0, core1,
    r1a, r1b, s2a, s2b, r2a, r2b, s3a, s3b, r3a, r3b,
    half_to, half_in, half_out, last_in,
    wsem, swap_s, swap_r, core_s, core_r, ag_s, ag_r, fw_s, fw_r, pc_s, pc_r, rs_s, rs_r, last_s, last_r, z_s, z_r,
):
    e = lax.axis_index("expert")
    d = lax.axis_index("dp")
    x, z = e // 4, lax.rem(e, 4)
    y, c = d // 2, lax.rem(d, 2)

    def shift(value, by):
        return lax.rem(value + by, 4)

    def device(px, pz, py, pc):
        return (px * 4 + pz, py * 2 + pc)

    other = device(x, z, y, 1 - c)
    along = {
        "x": lambda i: device(shift(x, i), z, y, c),
        "z": lambda i: device(x, shift(z, i), y, c),
        "y": lambda i: device(x, z, shift(y, i), c),
    }

    def remote(src, dst, ss, rs, dev):
        return pltpu.make_async_remote_copy(
            src_ref=src, dst_ref=dst, send_sem=ss, recv_sem=rs,
            device_id=dev, device_id_type=MESH,
        )

    loads = [
        pltpu.make_async_copy(gw.at[0], wg, wsem.at[0]),
        pltpu.make_async_copy(uw.at[0], wu, wsem.at[1]),
        pltpu.make_async_copy(dw.at[0], wd, wsem.at[2]),
    ]
    for cp in loads:
        cp.start()

    barrier = pltpu.get_barrier_semaphore()
    peers = [other] + [along[a](i) for a in "xzy" for i in (1, 2, 3)]
    for dev in peers:
        pl.semaphore_signal(barrier, inc=1, device_id=dev, device_id_type=MESH)

    wide = tok[...].astype(F32)
    named, level = routes[...], gates[...].astype(F32)
    slot = lax.broadcasted_iota(jnp.int32, (8, EXT), 1)
    by_expert = jnp.zeros((8, EXT), F32)
    for k in range(8):
        by_expert += jnp.where(named[:, k : k + 1] == slot, level[:, k : k + 1], 0.0)
    low, high = wide[:, 0 : 2 * Q], wide[:, 2 * Q :]
    half_to[:, 0 : 2 * Q] = jnp.where(c == 0, high, low)
    half_to[:, 2 * Q :] = by_expert
    own = jnp.concatenate([jnp.where(c == 0, low, high), by_expert], axis=1)
    pl.semaphore_wait(barrier, len(peers))

    def slab_piece(k, part):
        src, dst = ((gw, rg), (dw, rd))[k]
        rows = src.shape[1] // PIECES
        at = (0, pl.ds(part * rows, rows))
        return remote(src.at[at], dst.at[at], swap_s.at[k, part], swap_r.at[k, part], along["x"](2))

    swaps = [slab_piece(k, part) for k in range(2) for part in range(PIECES)]
    waiting = list(swaps)

    def send_pieces(number):
        for cp in waiting[:number]:
            cp.start()
        del waiting[:number]

    send_pieces(FIRST)

    first = remote(half_to, half_in, core_s.at[0], core_r.at[0], other)
    first.start()

    first.wait()
    got = half_in[...]
    block = jnp.where(
        c == 0, jnp.concatenate([own, got], axis=0), jnp.concatenate([got, own], axis=0)
    ).astype(BF)
    rows16 = pl.ds(pl.multiple_of(x * 16, 16), 16)
    x0[y, z, rows16, 0:Q] = block[:, 0:Q]
    x0[y, z, rows16, Q:W0] = block[:, 2 * Q : 2 * Q + EXT]
    x1[y, z, rows16, :] = block[:, Q : 2 * Q]

    sent = []

    def gather(stream, stage, i, buf, view, axis):
        cp = remote(
            buf.at[view], buf.at[view], ag_s.at[stream, stage, i - 1], ag_r.at[stream, stage, i - 1],
            along[axis](i),
        )
        cp.start()
        sent.append(cp)

    def landed(stream, stage, i, buf, view):
        remote(
            buf.at[view], buf.at[view], ag_s.at[stream, stage, i - 1], ag_r.at[stream, stage, i - 1], other
        ).wait_recv()

    for i in (1, 2, 3):
        gather(0, 0, i, x0, (y, z, rows16), "x")
        gather(1, 0, i, x1, (y, z, rows16), "x")
    send_pieces(SECOND)

    for i in (1, 2, 3):
        from16 = pl.ds(pl.multiple_of(shift(x, 4 - i) * 16, 16), 16)
        landed(0, 0, i, x0, (y, z, from16))
        landed(1, 0, i, x1, (y, z, from16))

    def block_at(stream, first, second):
        if stream == 0:
            return (shift(y, second), shift(z, first))
        return (shift(y, first), shift(z, second))

    def spread(stream, j):
        buf, axis = ((x0, "y"), (x1, "z"))[stream]
        view = block_at(stream, j, 0)
        for i in (1, 3, 2):
            cp = remote(
                buf.at[view], buf.at[view],
                last_s.at[stream, i - 1, j], last_r.at[stream, i - 1, j], along[axis](i),
            )
            cp.start()
            sent.append(cp)

    for i in (1, 3, 2):
        gather(0, 1, i, x0, (y, z), "z")
        gather(1, 1, i, x1, (y, z), "y")
    spread(0, 0)
    spread(1, 0)
    for i in (1, 3, 2):
        landed(0, 1, i, x0, block_at(0, 4 - i, 0))
        spread(0, 4 - i)
        landed(1, 1, i, x1, block_at(1, 4 - i, 0))
        spread(1, 4 - i)

    every = slice(None)
    forwards = []

    def forward(stream, i, view):
        src, dst = ((x0, o0), (x1, o1))[stream]
        cp = remote(src.at[view], dst.at[view], fw_s.at[stream, i], fw_r.at[stream, i], other)
        cp.start()
        forwards.append(cp)

    forward(0, 0, (y,))
    forward(1, 0, (every, z))
    for i in (1, 3, 2):
        for stream, buf in ((0, x0), (1, x1)):
            for j in range(4):
                view = block_at(stream, j, 4 - i)
                remote(
                    buf.at[view], buf.at[view],
                    last_s.at[stream, i - 1, j], last_r.at[stream, i - 1, j], other,
                ).wait_recv()
        forward(0, i, (shift(y, 4 - i),))
        forward(1, i, (every, shift(z, 4 - i)))
    for cp in forwards:
        cp.wait()
    for cp in sent:
        cp.wait_send()
    for cp in loads:
        cp.wait()

    lane = lax.broadcasted_iota(jnp.int32, (128, EXT), 1)
    lo = pl.multiple_of(c * 2 * Q, 2 * Q)
    hi = pl.multiple_of((1 - c) * 2 * Q, 2 * Q)

    def rows_of(ref, a, b):
        return ref[a, pl.ds(b * 2, 2)].reshape(128, ref.shape[-1])

    def turn(t, carry):
        a, b = t // 2, lax.rem(t, 2)
        full = rows_of(x0, a, b)
        parts = (
            (full[:, 0:Q], lo),
            (rows_of(x1, a, b), lo + Q),
            (rows_of(o0, a, b)[:, 0:Q], hi),
            (rows_of(o1, a, b), hi + Q),
        )
        gate = jnp.zeros((128, 256), F32)
        up = jnp.zeros((128, 256), F32)
        for part, start in parts:
            at = pl.ds(pl.multiple_of(start, Q), Q)
            gate += jnp.dot(part, wg[at, :], preferred_element_type=F32)
            up += jnp.dot(part, wu[at, :], preferred_element_type=F32)
        gate = gate * D ** (-0.5)
        up = up * D ** (-0.5)
        hidden = (gate / (1.0 + jnp.exp(-gate)) * up).astype(BF)
        weight = jnp.sum(
            jnp.where(lane == e, full[:, Q:W0].astype(F32), 0.0), axis=1, keepdims=True
        ) * FF ** (-0.5)
        for dst, start in ((send0, hi), (send1, hi + Q), (mine0, lo), (mine1, lo + Q)):
            at = pl.ds(pl.multiple_of(start, Q), Q)
            value = jnp.dot(hidden, wd[:, at], preferred_element_type=F32) * weight
            dst[a, pl.ds(b * 2, 2)] = value.astype(BF).reshape(2, 64, Q)
        return carry

    def part_copy(stream, a):
        src, dst = ((send0, core0), (send1, core1))[stream]
        return remote(src.at[a], dst.at[a], pc_s.at[stream, a], pc_r.at[stream, a], other)

    out_copies = []

    def scatter(stream, stage, i, src, dst, axis):
        cp = remote(src, dst, rs_s.at[stream, stage, i - 1], rs_r.at[stream, stage, i - 1], along[axis](i))
        cp.start()
        out_copies.append(cp)
        return cp

    def total(own_value, got_ref, at=()):
        value = own_value.astype(F32)
        for i in range(3):
            value += got_ref[(i,) + at].astype(F32)
        return value

    def first_y(p):
        return remote(
            mine0.at[shift(y, p + 1)], r1a.at[p], rs_s.at[0, 0, p], rs_r.at[0, 0, p], along["y"](p + 1)
        )

    def first_z(p, i):
        a = shift(y, p + 1)
        return remote(
            mine1.at[a, shift(z, i)], r1b.at[i - 1, a], z_s.at[i - 1, p], z_r.at[i - 1, p], along["z"](i)
        )

    def quarter(q, carry):
        @pl.when(q < 4)
        def _():
            a = shift(y, q + 1)
            lax.fori_loop(2 * a, 2 * a + 2, turn, 0)
            part_copy(0, a).start()
            part_copy(1, a).start()

        @pl.when(q > 0)
        def _():
            p = q - 1
            a = shift(y, p + 1)
            part_copy(0, a).wait()
            part_copy(1, a).wait()
            for own_ref, got_ref in ((mine0, core0), (mine1, core1)):
                for b in range(4):
                    own_ref[a, b] = (own_ref[a, b].astype(F32) + got_ref[a, b].astype(F32)).astype(BF)
            for i in (1, 3, 2):
                first_z(p, i).start()

            @pl.when(p < 3)
            def _():
                first_y(p).start()

        return carry

    lax.fori_loop(0, 5, quarter, 0)
    send_pieces(THIRD)

    def first_landed(p, carry):
        for i in (1, 2, 3):
            first_z(p, i).wait()
        return carry

    lax.fori_loop(0, 4, first_landed, 0)
    for p in range(3):
        first_y(p).wait()
    for b in range(4):
        s2a[b] = total(mine0[y, b], r1a, (b,)).astype(BF)
        s2b[b] = total(mine1[b, z], r1b, (b,)).astype(BF)
    stage = []
    for i in (1, 2, 3):
        stage.append(scatter(0, 1, i, s2a.at[shift(z, i)], r2a.at[i - 1], "z"))
        stage.append(scatter(1, 1, i, s2b.at[shift(y, i)], r2b.at[i - 1], "y"))
    send_pieces(FOURTH)
    for cp in stage:
        cp.wait_recv()
    s3a[...] = total(s2a[z], r2a).astype(BF)
    s3b[...] = total(s2b[y], r2b).astype(BF)
    stage = []
    for i in (1, 2, 3):
        to16 = pl.ds(pl.multiple_of(shift(x, i) * 16, 16), 16)
        stage.append(scatter(0, 2, i, s3a.at[to16], r3a.at[i - 1], "x"))
        stage.append(scatter(1, 2, i, s3b.at[to16], r3b.at[i - 1], "x"))
    send_pieces(len(waiting))
    for cp in stage:
        cp.wait_recv()
    sum_a = total(s3a[rows16, :], r3a)
    sum_b = total(s3b[rows16, :], r3b)
    keep_a = jnp.where(c == 0, sum_a[0:8], sum_a[8:16])
    keep_b = jnp.where(c == 0, sum_b[0:8], sum_b[8:16])
    half_out[:, 0:Q] = jnp.where(c == 0, sum_a[8:16], sum_a[0:8])
    half_out[:, Q : 2 * Q] = jnp.where(c == 0, sum_b[8:16], sum_b[0:8])
    last = remote(half_out, last_in, core_s.at[1], core_r.at[1], other)
    last.start()
    last.wait()
    kept = jnp.concatenate([keep_a, keep_b], axis=1)
    given = last_in[...]
    out[:, 0 : 2 * Q] = jnp.where(c == 0, kept, given).astype(BF)
    out[:, 2 * Q :] = jnp.where(c == 0, given, kept).astype(BF)

    for cp in out_copies:
        cp.wait_send()
    for cp in swaps:
        cp.wait()


def moe(tok, routes, gates, gate_weight, up_weight, down_weight):
    vm = lambda *shape: pltpu.VMEM(shape, BF)
    dma = lambda *shape: pltpu.SemaphoreType.DMA(shape)
    any_spec = pl.BlockSpec(memory_space=pl.ANY)
    vmem_spec = pl.BlockSpec(memory_space=pltpu.VMEM)
    like = lambda a: jax.ShapeDtypeStruct(a.shape, a.dtype)
    return pl.pallas_call(
        moe_kernel,
        out_shape=(
            jax.ShapeDtypeStruct((8, D), BF),
            like(gate_weight), like(down_weight),
        ),
        in_specs=[vmem_spec] * 3 + [any_spec] * 3,
        out_specs=(vmem_spec, any_spec, any_spec),
        scratch_shapes=[
            vm(4, 4, 64, W0), vm(4, 4, 64, Q), vm(4, 4, 64, W0), vm(4, 4, 64, Q),
            vm(D, 256), vm(D, 256), vm(256, D),
            vm(4, 4, 64, Q), vm(4, 4, 64, Q), vm(4, 4, 64, Q), vm(4, 4, 64, Q),
            vm(4, 4, 64, Q), vm(4, 4, 64, Q),
            vm(3, 4, 64, Q), vm(3, 4, 64, Q), vm(4, 64, Q), vm(4, 64, Q),
            vm(3, 64, Q), vm(3, 64, Q), vm(64, Q), vm(64, Q), vm(3, 16, Q), vm(3, 16, Q),
            pltpu.VMEM((8, 2 * Q + EXT), F32), pltpu.VMEM((8, 2 * Q + EXT), F32),
            pltpu.VMEM((8, 2 * Q), F32), pltpu.VMEM((8, 2 * Q), F32),
            dma(3), dma(2, PIECES), dma(2, PIECES), dma(2), dma(2),
            dma(2, 3, 3), dma(2, 3, 3), dma(2, 4), dma(2, 4), dma(2, 4), dma(2, 4),
            dma(2, 3, 3), dma(2, 3, 3),
            dma(2, 3, 4), dma(2, 3, 4), dma(3, 4), dma(3, 4),
        ],
        compiler_params=pltpu.CompilerParams(
            collective_id=0, has_side_effects=True, vmem_limit_bytes=64 * 1024 * 1024
        ),
        cost_estimate=pl.CostEstimate(
            flops=6 * 1024 * D * 256, bytes_accessed=33 * 1024 * 1024, transcendentals=1024 * 256
        ),
        name="moe_and_exchange",
    )(tok, routes, gates, gate_weight, up_weight, down_weight)


def pick_kernel(swapped, og, ou, od, rg, ru, rd, mg, mu, md, bg, bu, bd, in_sem, out_sem):
    outs, bufs = (mg, mu, md), (bg, bu, bd)
    flag = swapped[lax.rem(lax.axis_index("expert"), EXPERTS // 2)]

    def go(sources):
        loads, stores = [], []
        for part in range(PIECES):
            for k, (src, buf, dst) in enumerate(zip(sources, bufs, outs)):
                rows = src.shape[1] // PIECES
                at = pl.ds(part * rows, rows)
                loads.append(pltpu.make_async_copy(src.at[0, at], buf.at[at], in_sem.at[k, part]))
                stores.append(pltpu.make_async_copy(buf.at[at], dst.at[0, at], out_sem.at[k, part]))
        for cp in loads:
            cp.start()
        for load, store in zip(loads, stores):
            load.wait()
            store.start()
        for cp in stores:
            cp.wait()

    @pl.when(flag == 1)
    def _():
        go((rg, ru, rd))

    @pl.when(flag != 1)
    def _():
        go((og, ou, od))


def pick(swapped, own, received):
    any_spec = pl.BlockSpec(memory_space=pl.ANY)
    return pl.pallas_call(
        pick_kernel,
        out_shape=tuple(jax.ShapeDtypeStruct(a.shape, a.dtype) for a in own),
        in_specs=[pl.BlockSpec(memory_space=pltpu.SMEM)] + [any_spec] * 6,
        out_specs=(any_spec,) * 3,
        scratch_shapes=[pltpu.VMEM(a.shape[1:], a.dtype) for a in own]
        + [pltpu.SemaphoreType.DMA((3, PIECES)), pltpu.SemaphoreType.DMA((3, PIECES))],
        compiler_params=pltpu.CompilerParams(vmem_limit_bytes=64 * 1024 * 1024),
        name="pick_slab",
    )(swapped, *own, *received)


def on_device(tokens, routes, gates, swapped, gate_weight, up_weight, down_weight):
    mixed, got_gate, got_down = moe(tokens, routes, gates, gate_weight, up_weight, down_weight)
    up_slab, got_gate, got_down = lax.optimization_barrier((up_weight, got_gate, got_down))
    bits = jnp.sum(swapped[1:] * 2 ** jnp.arange(7, dtype=jnp.int32))
    number = jnp.array(SERVES, jnp.int32)[bits]
    got_up = lax.switch(number, [functools.partial(exchange, p) for p in SETS], up_slab)
    moved = pick(swapped, (gate_weight, up_weight, down_weight), (got_gate, got_up, got_down))
    return (mixed, *moved)


def solution(mesh):
    in_specs = (
        P(("expert", "dp"), None),
        P(("expert", "dp"), None),
        P(("expert", "dp"), None),
        P(),
        P("expert", None, "dp"),
        P("expert", None, "dp"),
        P("expert", "dp", None),
    )
    out_specs = (
        P(("expert", "dp"), None),
        P("expert", None, "dp"),
        P("expert", None, "dp"),
        P("expert", "dp", None),
    )
    return jax.shard_map(
        on_device, mesh=mesh, in_specs=in_specs, out_specs=out_specs, check_vma=False
    )
```

```python
import functools

import jax
import jax.numpy as jnp
from jax import lax
from jax.experimental import pallas as pl
from jax.experimental.pallas import tpu as pltpu
from jax.sharding import PartitionSpec as P

D = 7168
FF = 2048
EXPERTS = 16
Q = D // 4
EXT = 128
W0 = Q + EXT
BF = jnp.bfloat16
F32 = jnp.float32
MESH = pl.DeviceIdType.MESH
PIECES = 8
FIRST, SECOND, THIRD, FOURTH = 1, 11, 2, 1

CHUNKS = 8
UNIT = 16

ROUTES = {
    15: ((1, 29), (0, 27), (11, 29), (10, 27), (21, 29), (20, 27), (31, 29), (30, 27)),
    41: ((1, 22), (0, 20), (3, 7), (5, 7), (29, 13), (31, 23), (30, 20), (43, 23), (42, 13), (45, 20)),
    51: ((1, 29), (7, 27), (11, 29), (13, 27), (33, 29), (39, 27), (43, 29), (45, 27)),
    61: ((1, 36), (3, 20), (19, 13), (21, 36), (20, 7), (31, 36), (30, 20), (33, 36), (37, 7), (39, 13), (43, 36), (45, 20)),
    85: ((1, 29), (3, 27), (21, 29), (23, 27), (33, 29), (35, 27), (53, 29), (55, 27)),
    103: ((1, 36), (0, 20), (8, 6), (11, 37), (15, 13), (21, 36), (23, 20), (41, 6), (43, 37), (47, 13), (53, 36), (55, 20)),
    107: ((1, 36), (0, 20), (11, 36), (13, 20), (29, 13), (31, 36), (30, 7), (41, 13), (43, 36), (47, 7), (53, 36), (55, 20)),
    119: ((1, 43), (7, 13), (11, 43), (15, 13), (21, 43), (23, 13), (33, 43), (39, 13), (43, 43), (47, 13), (53, 43), (55, 13)),
    127: ((1, 50), (6, 6), (11, 50), (14, 6), (21, 50), (22, 6), (31, 50), (30, 6), (33, 50), (39, 6), (43, 50), (47, 6), (53, 50), (55, 6)),
    151: ((1, 36), (7, 20), (11, 36), (10, 20), (21, 36), (20, 20), (33, 36), (35, 13), (37, 7), (61, 7), (63, 36), (62, 13)),
    153: ((1, 29), (3, 27), (29, 27), (31, 29), (33, 29), (35, 27), (61, 27), (63, 29)),
    165: ((1, 29), (3, 27), (21, 29), (23, 27), (43, 29), (45, 27), (57, 27), (63, 29)),
    171: ((1, 36), (0, 20), (8, 6), (11, 37), (13, 13), (29, 20), (31, 36), (41, 6), (43, 37), (45, 13), (61, 20), (63, 36)),
    187: ((1, 43), (5, 13), (11, 43), (13, 13), (29, 13), (31, 43), (33, 43), (37, 13), (43, 43), (45, 13), (61, 13), (63, 43)),
    195: ((1, 29), (0, 27), (11, 29), (13, 27), (51, 27), (53, 29), (63, 29), (62, 27)),
    205: ((1, 36), (0, 20), (19, 20), (21, 36), (24, 6), (27, 13), (31, 37), (51, 20), (53, 36), (57, 6), (59, 13), (63, 37)),
    219: ((1, 43), (5, 13), (11, 43), (10, 13), (29, 13), (31, 43), (33, 43), (35, 13), (53, 43), (52, 13), (59, 13), (63, 43)),
    221: ((1, 43), (3, 13), (19, 13), (21, 43), (27, 13), (31, 43), (33, 43), (35, 13), (51, 13), (53, 43), (59, 13), (63, 43)),
    231: ((1, 43), (7, 13), (11, 43), (15, 13), (21, 43), (23, 13), (41, 13), (43, 43), (49, 13), (53, 43), (57, 13), (63, 43)),
    237: ((1, 43), (3, 13), (19, 13), (21, 43), (27, 13), (31, 43), (41, 13), (43, 43), (49, 13), (53, 43), (57, 13), (63, 43)),
    239: ((1, 50), (0, 6), (8, 6), (11, 50), (16, 6), (21, 50), (24, 6), (31, 50), (41, 6), (43, 50), (49, 6), (53, 50), (57, 6), (63, 50)),
    241: ((1, 36), (3, 6), (7, 14), (33, 37), (34, 7), (36, 12), (43, 36), (42, 20), (53, 36), (52, 20), (63, 36), (62, 20)),
    247: ((1, 50), (7, 6), (11, 50), (15, 6), (21, 50), (23, 6), (33, 50), (38, 6), (43, 50), (46, 6), (53, 50), (54, 6), (63, 50), (62, 6)),
    255: ((1, 56), (11, 56), (21, 56), (31, 56), (33, 56), (43, 56), (53, 56), (63, 56)),
}
SETS = sorted(ROUTES)
SERVES = (
    1, 0, 0, 0, 1, 0, 0, 0, 2, 2, 4, 9, 10, 13, 3, 8,
    1, 2, 11, 5, 1, 12, 3, 8, 2, 2, 3, 7, 3, 13, 3, 8,
    4, 14, 4, 5, 15, 6, 15, 8, 4, 7, 4, 7, 16, 16, 17, 8,
    5, 5, 5, 5, 6, 6, 19, 8, 21, 7, 7, 7, 8, 8, 8, 8,
    10, 14, 11, 9, 10, 12, 15, 20, 10, 9, 9, 9, 10, 13, 17, 23,
    11, 12, 11, 18, 12, 12, 19, 20, 21, 13, 22, 22, 13, 13, 23, 23,
    14, 14, 15, 18, 15, 16, 15, 20, 21, 16, 17, 22, 16, 16, 17, 23,
    21, 18, 18, 18, 19, 20, 19, 20, 21, 22, 22, 22, 23, 23, 23, 23,
)


def legs_of(z, ring, direct, sign):
    stops = [(0, z)]
    if ring != z:
        stops.append((0, ring))
    if not direct:
        stops.append((-sign, ring))
    stops.append((2, z))
    return list(zip(stops[:-1], stops[1:]))


class Leg:
    pass


def layout(pairs):
    lands, relay_rows = {}, {}
    legs = []
    base = {}
    for code, units in ROUTES[pairs]:
        parity, z, ring, direct = code // 32, code // 8 % 4, code // 2 % 4, code % 2
        rows = units * UNIT
        start = base.get((parity, z), 0)
        base[parity, z] = start + rows * CHUNKS
        before = None
        steps = legs_of(z, ring, direct, 1 - 2 * parity)
        for k, (a, b) in enumerate(steps):
            leg = Leg()
            leg.rows, leg.start, leg.before, leg.turn = rows, start, before, k
            leg.final = k == len(steps) - 1
            leg.move = (b[0] - a[0], b[1])
            leg.back = (a[0] - b[0], a[1])
            leg.sender = ((parity + a[0]) % 2, a[1])
            leg.taker = ((parity + b[0]) % 2, b[1])
            if not leg.final:
                leg.land_slot = lands.get(leg.taker, 0)
                lands[leg.taker] = leg.land_slot + 1
                leg.relay = relay_rows.get(leg.taker, 0)
                relay_rows[leg.taker] = leg.relay + rows * CHUNKS
            legs.append(leg)
            before = leg
    return legs, max(lands.values(), default=1), max(relay_rows.values(), default=UNIT)


def exchange_kernel(legs, src, dst, relay, end_sem, land_sem):
    e = lax.axis_index("expert")
    d = lax.axis_index("dp")
    x, z = e // 4, lax.rem(e, 4)

    def device(move):
        return (lax.rem(x + move[0] + 4, 4) * 4 + move[1], d)

    kinds = sorted({leg.sender for leg in legs} | {leg.taker for leg in legs})
    barrier = pltpu.get_barrier_semaphore()
    for kind in kinds:
        @pl.when((lax.rem(x, 2) == kind[0]) & (z == kind[1]))
        def _(kind=kind):
            peers = {(leg.move[0] % 4, leg.move[1]) for leg in legs if leg.sender == kind}
            peers |= {(leg.back[0] % 4, leg.back[1]) for leg in legs if leg.taker == kind}
            for move in sorted(peers):
                pl.semaphore_signal(barrier, inc=1, device_id=device(move), device_id_type=MESH)
            pl.semaphore_wait(barrier, len(peers))

    def own(leg, chunk):
        return pl.ds(pl.multiple_of(leg.start + chunk * leg.rows, UNIT), leg.rows)

    def spot(leg, chunk):
        if leg.final:
            return dst.at[0, own(leg, chunk)]
        return relay.at[pl.ds(pl.multiple_of(leg.relay + chunk * leg.rows, UNIT), leg.rows)]

    def copy(leg, chunk):
        return pltpu.make_async_remote_copy(
            src_ref=src.at[0, own(leg, chunk)] if leg.turn == 0 else spot(leg.before, chunk),
            dst_ref=spot(leg, chunk),
            send_sem=end_sem.at[min(leg.turn, 1)],
            recv_sem=end_sem.at[2] if leg.final else land_sem.at[leg.land_slot, chunk],
            device_id=device(leg.move), device_id_type=MESH,
        )

    def arrival(leg, chunk):
        here = spot(leg, chunk)
        return pltpu.make_async_remote_copy(
            src_ref=here, dst_ref=here,
            send_sem=end_sem.at[0],
            recv_sem=land_sem.at[leg.land_slot, chunk],
            device_id=device((2, z)), device_id_type=MESH,
        )

    def whole(ref):
        return pltpu.make_async_remote_copy(
            src_ref=ref, dst_ref=ref, send_sem=end_sem.at[0], recv_sem=end_sem.at[2],
            device_id=device((2, z)), device_id_type=MESH,
        )

    for kind in kinds:
        @pl.when((lax.rem(x, 2) == kind[0]) & (z == kind[1]))
        def _(kind=kind):
            out = [leg for leg in legs if leg.sender == kind]
            late = max([leg.turn for leg in out], default=0)

            def push(step, carry):
                for turn in range(late + 1):
                    chunk = step - turn

                    @pl.when((chunk >= 0) & (chunk < CHUNKS))
                    def _(turn=turn, chunk=chunk):
                        for leg in out:
                            if leg.turn == turn:
                                if turn:
                                    arrival(leg.before, chunk).wait_recv()
                                copy(leg, chunk).start()
                return carry

            if out:
                lax.fori_loop(0, CHUNKS + late, push, 0)
            passed = sum(leg.rows for leg in out if leg.turn) * CHUNKS
            if any(leg.final and leg.taker == kind for leg in legs):
                whole(dst.at[0]).wait_recv()
                whole(src.at[0]).wait_send()
            if passed:
                relayed = relay.at[pl.ds(0, passed)]
                pltpu.make_async_remote_copy(
                    src_ref=relayed, dst_ref=relayed,
                    send_sem=end_sem.at[1], recv_sem=end_sem.at[2],
                    device_id=device((2, z)), device_id_type=MESH,
                ).wait_send()


def exchange(pairs, weight):
    any_spec = pl.BlockSpec(memory_space=pl.ANY)
    legs, n_land, n_relay = layout(pairs)
    return pl.pallas_call(
        functools.partial(exchange_kernel, legs),
        out_shape=jax.ShapeDtypeStruct(weight.shape, weight.dtype),
        in_specs=[any_spec],
        out_specs=any_spec,
        scratch_shapes=[
            pltpu.VMEM((n_relay, 256), BF),
            pltpu.SemaphoreType.DMA((3,)),
            pltpu.SemaphoreType.DMA((n_land, CHUNKS)),
        ],
        compiler_params=pltpu.CompilerParams(
            collective_id=1 + pairs // 2, has_side_effects=True, vmem_limit_bytes=60 * 1024 * 1024
        ),
        cost_estimate=pl.CostEstimate(flops=0, bytes_accessed=64 * 1024 * 1024, transcendentals=0),
        name="exchange_%d" % pairs,
    )(weight)


def moe_kernel(
    swapped, tok, routes, gates, gw, uw, dw,
    out, rg, rd, number,
    x0, x1, o0, o1, wg, wu, wd,
    mine0, mine1, send0, send1, core0, core1,
    r1a, r1b, s2a, s2b, r2a, r2b, s3a, s3b, r3a, r3b,
    half_to, half_in, half_out, last_in,
    wsem, swap_s, swap_r, core_s, core_r, ag_s, ag_r, fw_s, fw_r, pc_s, pc_r, rs_s, rs_r, last_s, last_r, z_s, z_r,
):
    e = lax.axis_index("expert")
    d = lax.axis_index("dp")
    x, z = e // 4, lax.rem(e, 4)
    y, c = d // 2, lax.rem(d, 2)

    def shift(value, by):
        return lax.rem(value + by, 4)

    def device(px, pz, py, pc):
        return (px * 4 + pz, py * 2 + pc)

    other = device(x, z, y, 1 - c)
    along = {
        "x": lambda i: device(shift(x, i), z, y, c),
        "z": lambda i: device(x, shift(z, i), y, c),
        "y": lambda i: device(x, z, shift(y, i), c),
    }

    def remote(src, dst, ss, rs, dev):
        return pltpu.make_async_remote_copy(
            src_ref=src, dst_ref=dst, send_sem=ss, recv_sem=rs,
            device_id=dev, device_id_type=MESH,
        )

    bits = swapped[1]
    for k in range(2, 8):
        bits += swapped[k] * 2 ** (k - 1)
    serving = jnp.int32(0)
    for n, serves in enumerate(SERVES):
        serving += jnp.where(bits == n, serves, 0)
    number[0] = serving

    loads = [
        pltpu.make_async_copy(gw.at[0], wg, wsem.at[0]),
        pltpu.make_async_copy(uw.at[0], wu, wsem.at[1]),
        pltpu.make_async_copy(dw.at[0], wd, wsem.at[2]),
    ]
    for cp in loads:
        cp.start()

    barrier = pltpu.get_barrier_semaphore()
    peers = [other] + [along[a](i) for a in "xzy" for i in (1, 2, 3)]
    for dev in peers:
        pl.semaphore_signal(barrier, inc=1, device_id=dev, device_id_type=MESH)

    wide = tok[...].astype(F32)
    named, level = routes[...], gates[...].astype(F32)
    slot = lax.broadcasted_iota(jnp.int32, (8, EXT), 1)
    by_expert = jnp.zeros((8, EXT), F32)
    for k in range(8):
        by_expert += jnp.where(named[:, k : k + 1] == slot, level[:, k : k + 1], 0.0)
    low, high = wide[:, 0 : 2 * Q], wide[:, 2 * Q :]
    half_to[:, 0 : 2 * Q] = jnp.where(c == 0, high, low)
    half_to[:, 2 * Q :] = by_expert
    own = jnp.concatenate([jnp.where(c == 0, low, high), by_expert], axis=1)
    pl.semaphore_wait(barrier, len(peers))

    def slab_piece(k, part):
        src, dst = ((gw, rg), (dw, rd))[k]
        rows = src.shape[1] // PIECES
        at = (0, pl.ds(part * rows, rows))
        return remote(src.at[at], dst.at[at], swap_s.at[k, part], swap_r.at[k, part], along["x"](2))

    swaps = [slab_piece(k, part) for k in range(2) for part in range(PIECES)]
    waiting = list(swaps)

    def send_pieces(number):
        for cp in waiting[:number]:
            cp.start()
        del waiting[:number]

    send_pieces(FIRST)

    first = remote(half_to, half_in, core_s.at[0], core_r.at[0], other)
    first.start()

    first.wait()
    got = half_in[...]
    block = jnp.where(
        c == 0, jnp.concatenate([own, got], axis=0), jnp.concatenate([got, own], axis=0)
    ).astype(BF)
    rows16 = pl.ds(pl.multiple_of(x * 16, 16), 16)
    x0[y, z, rows16, 0:Q] = block[:, 0:Q]
    x0[y, z, rows16, Q:W0] = block[:, 2 * Q : 2 * Q + EXT]
    x1[y, z, rows16, :] = block[:, Q : 2 * Q]

    sent = []

    def gather(stream, stage, i, buf, view, axis):
        cp = remote(
            buf.at[view], buf.at[view], ag_s.at[stream, stage, i - 1], ag_r.at[stream, stage, i - 1],
            along[axis](i),
        )
        cp.start()
        sent.append(cp)

    def landed(stream, stage, i, buf, view):
        remote(
            buf.at[view], buf.at[view], ag_s.at[stream, stage, i - 1], ag_r.at[stream, stage, i - 1], other
        ).wait_recv()

    for i in (1, 2, 3):
        gather(0, 0, i, x0, (y, z, rows16), "x")
        gather(1, 0, i, x1, (y, z, rows16), "x")
    send_pieces(SECOND)

    for i in (1, 2, 3):
        from16 = pl.ds(pl.multiple_of(shift(x, 4 - i) * 16, 16), 16)
        landed(0, 0, i, x0, (y, z, from16))
        landed(1, 0, i, x1, (y, z, from16))

    def block_at(stream, first, second):
        if stream == 0:
            return (shift(y, second), shift(z, first))
        return (shift(y, first), shift(z, second))

    def spread(stream, j):
        buf, axis = ((x0, "y"), (x1, "z"))[stream]
        view = block_at(stream, j, 0)
        for i in (1, 3, 2):
            cp = remote(
                buf.at[view], buf.at[view],
                last_s.at[stream, i - 1, j], last_r.at[stream, i - 1, j], along[axis](i),
            )
            cp.start()
            sent.append(cp)

    for i in (1, 3, 2):
        gather(0, 1, i, x0, (y, z), "z")
        gather(1, 1, i, x1, (y, z), "y")
    spread(0, 0)
    spread(1, 0)
    for i in (1, 3, 2):
        landed(0, 1, i, x0, block_at(0, 4 - i, 0))
        spread(0, 4 - i)
        landed(1, 1, i, x1, block_at(1, 4 - i, 0))
        spread(1, 4 - i)

    every = slice(None)
    forwards = []

    def forward(stream, i, view):
        src, dst = ((x0, o0), (x1, o1))[stream]
        cp = remote(src.at[view], dst.at[view], fw_s.at[stream, i], fw_r.at[stream, i], other)
        cp.start()
        forwards.append(cp)

    forward(0, 0, (y,))
    forward(1, 0, (every, z))
    for i in (1, 3, 2):
        for stream, buf in ((0, x0), (1, x1)):
            for j in range(4):
                view = block_at(stream, j, 4 - i)
                remote(
                    buf.at[view], buf.at[view],
                    last_s.at[stream, i - 1, j], last_r.at[stream, i - 1, j], other,
                ).wait_recv()
        forward(0, i, (shift(y, 4 - i),))
        forward(1, i, (every, shift(z, 4 - i)))
    for cp in forwards:
        cp.wait()
    for cp in sent:
        cp.wait_send()
    for cp in loads:
        cp.wait()

    lane = lax.broadcasted_iota(jnp.int32, (128, EXT), 1)
    lo = pl.multiple_of(c * 2 * Q, 2 * Q)
    hi = pl.multiple_of((1 - c) * 2 * Q, 2 * Q)

    def rows_of(ref, a, b):
        return ref[a, pl.ds(b * 2, 2)].reshape(128, ref.shape[-1])

    def turn(t, carry):
        a, b = t // 2, lax.rem(t, 2)
        full = rows_of(x0, a, b)
        parts = (
            (full[:, 0:Q], lo),
            (rows_of(x1, a, b), lo + Q),
            (rows_of(o0, a, b)[:, 0:Q], hi),
            (rows_of(o1, a, b), hi + Q),
        )
        gate = jnp.zeros((128, 256), F32)
        up = jnp.zeros((128, 256), F32)
        for part, start in parts:
            at = pl.ds(pl.multiple_of(start, Q), Q)
            gate += jnp.dot(part, wg[at, :], preferred_element_type=F32)
            up += jnp.dot(part, wu[at, :], preferred_element_type=F32)
        gate = gate * D ** (-0.5)
        up = up * D ** (-0.5)
        hidden = (gate / (1.0 + jnp.exp(-gate)) * up).astype(BF)
        weight = jnp.sum(
            jnp.where(lane == e, full[:, Q:W0].astype(F32), 0.0), axis=1, keepdims=True
        ) * FF ** (-0.5)
        for dst, start in ((send0, hi), (send1, hi + Q), (mine0, lo), (mine1, lo + Q)):
            at = pl.ds(pl.multiple_of(start, Q), Q)
            value = jnp.dot(hidden, wd[:, at], preferred_element_type=F32) * weight
            dst[a, pl.ds(b * 2, 2)] = value.astype(BF).reshape(2, 64, Q)
        return carry

    def part_copy(stream, a):
        src, dst = ((send0, core0), (send1, core1))[stream]
        return remote(src.at[a], dst.at[a], pc_s.at[stream, a], pc_r.at[stream, a], other)

    out_copies = []

    def scatter(stream, stage, i, src, dst, axis):
        cp = remote(src, dst, rs_s.at[stream, stage, i - 1], rs_r.at[stream, stage, i - 1], along[axis](i))
        cp.start()
        out_copies.append(cp)
        return cp

    def total(own_value, got_ref, at=()):
        value = own_value.astype(F32)
        for i in range(3):
            value += got_ref[(i,) + at].astype(F32)
        return value

    def first_y(p):
        return remote(
            mine0.at[shift(y, p + 1)], r1a.at[p], rs_s.at[0, 0, p], rs_r.at[0, 0, p], along["y"](p + 1)
        )

    def first_z(p, i):
        a = shift(y, p + 1)
        return remote(
            mine1.at[a, shift(z, i)], r1b.at[i - 1, a], z_s.at[i - 1, p], z_r.at[i - 1, p], along["z"](i)
        )

    def quarter(q, carry):
        @pl.when(q < 4)
        def _():
            a = shift(y, q + 1)
            lax.fori_loop(2 * a, 2 * a + 2, turn, 0)
            part_copy(0, a).start()
            part_copy(1, a).start()

        @pl.when(q > 0)
        def _():
            p = q - 1
            a = shift(y, p + 1)
            part_copy(0, a).wait()
            part_copy(1, a).wait()
            for own_ref, got_ref in ((mine0, core0), (mine1, core1)):
                for b in range(4):
                    own_ref[a, b] = (own_ref[a, b].astype(F32) + got_ref[a, b].astype(F32)).astype(BF)
            for i in (1, 3, 2):
                first_z(p, i).start()

            @pl.when(p < 3)
            def _():
                first_y(p).start()

        return carry

    lax.fori_loop(0, 5, quarter, 0)
    send_pieces(THIRD)

    def first_landed(p, carry):
        for i in (1, 2, 3):
            first_z(p, i).wait()
        return carry

    lax.fori_loop(0, 4, first_landed, 0)
    for p in range(3):
        first_y(p).wait()
    for b in range(4):
        s2a[b] = total(mine0[y, b], r1a, (b,)).astype(BF)
        s2b[b] = total(mine1[b, z], r1b, (b,)).astype(BF)
    stage = []
    for i in (1, 2, 3):
        stage.append(scatter(0, 1, i, s2a.at[shift(z, i)], r2a.at[i - 1], "z"))
        stage.append(scatter(1, 1, i, s2b.at[shift(y, i)], r2b.at[i - 1], "y"))
    send_pieces(FOURTH)
    for cp in stage:
        cp.wait_recv()
    s3a[...] = total(s2a[z], r2a).astype(BF)
    s3b[...] = total(s2b[y], r2b).astype(BF)
    stage = []
    for i in (1, 2, 3):
        to16 = pl.ds(pl.multiple_of(shift(x, i) * 16, 16), 16)
        stage.append(scatter(0, 2, i, s3a.at[to16], r3a.at[i - 1], "x"))
        stage.append(scatter(1, 2, i, s3b.at[to16], r3b.at[i - 1], "x"))
    send_pieces(len(waiting))
    for cp in stage:
        cp.wait_recv()
    sum_a = total(s3a[rows16, :], r3a)
    sum_b = total(s3b[rows16, :], r3b)
    keep_a = jnp.where(c == 0, sum_a[0:8], sum_a[8:16])
    keep_b = jnp.where(c == 0, sum_b[0:8], sum_b[8:16])
    half_out[:, 0:Q] = jnp.where(c == 0, sum_a[8:16], sum_a[0:8])
    half_out[:, Q : 2 * Q] = jnp.where(c == 0, sum_b[8:16], sum_b[0:8])
    last = remote(half_out, last_in, core_s.at[1], core_r.at[1], other)
    last.start()
    last.wait()
    kept = jnp.concatenate([keep_a, keep_b], axis=1)
    given = last_in[...]
    out[:, 0 : 2 * Q] = jnp.where(c == 0, kept, given).astype(BF)
    out[:, 2 * Q :] = jnp.where(c == 0, given, kept).astype(BF)

    for cp in out_copies:
        cp.wait_send()
    for cp in swaps:
        cp.wait()


def moe(swapped, tok, routes, gates, gate_weight, up_weight, down_weight):
    vm = lambda *shape: pltpu.VMEM(shape, BF)
    dma = lambda *shape: pltpu.SemaphoreType.DMA(shape)
    any_spec = pl.BlockSpec(memory_space=pl.ANY)
    vmem_spec = pl.BlockSpec(memory_space=pltpu.VMEM)
    smem_spec = pl.BlockSpec(memory_space=pltpu.SMEM)
    like = lambda a: jax.ShapeDtypeStruct(a.shape, a.dtype)
    return pl.pallas_call(
        moe_kernel,
        out_shape=(
            jax.ShapeDtypeStruct((8, D), BF),
            like(gate_weight), like(down_weight),
            jax.ShapeDtypeStruct((1,), jnp.int32),
        ),
        in_specs=[smem_spec] + [vmem_spec] * 3 + [any_spec] * 3,
        out_specs=(vmem_spec, any_spec, any_spec, smem_spec),
        scratch_shapes=[
            vm(4, 4, 64, W0), vm(4, 4, 64, Q), vm(4, 4, 64, W0), vm(4, 4, 64, Q),
            vm(D, 256), vm(D, 256), vm(256, D),
            vm(4, 4, 64, Q), vm(4, 4, 64, Q), vm(4, 4, 64, Q), vm(4, 4, 64, Q),
            vm(4, 4, 64, Q), vm(4, 4, 64, Q),
            vm(3, 4, 64, Q), vm(3, 4, 64, Q), vm(4, 64, Q), vm(4, 64, Q),
            vm(3, 64, Q), vm(3, 64, Q), vm(64, Q), vm(64, Q), vm(3, 16, Q), vm(3, 16, Q),
            pltpu.VMEM((8, 2 * Q + EXT), F32), pltpu.VMEM((8, 2 * Q + EXT), F32),
            pltpu.VMEM((8, 2 * Q), F32), pltpu.VMEM((8, 2 * Q), F32),
            dma(3), dma(2, PIECES), dma(2, PIECES), dma(2), dma(2),
            dma(2, 3, 3), dma(2, 3, 3), dma(2, 4), dma(2, 4), dma(2, 4), dma(2, 4),
            dma(2, 3, 3), dma(2, 3, 3),
            dma(2, 3, 4), dma(2, 3, 4), dma(3, 4), dma(3, 4),
        ],
        compiler_params=pltpu.CompilerParams(
            collective_id=0, has_side_effects=True, vmem_limit_bytes=64 * 1024 * 1024
        ),
        cost_estimate=pl.CostEstimate(
            flops=6 * 1024 * D * 256, bytes_accessed=33 * 1024 * 1024, transcendentals=1024 * 256
        ),
        name="moe_and_exchange",
    )(swapped, tok, routes, gates, gate_weight, up_weight, down_weight)


def pick_kernel(swapped, mixed, og, ou, od, rg, ru, rd, out, mg, mu, md, bg, bu, bd, in_sem, out_sem):
    out[...] = mixed[...]
    outs, bufs = (mg, mu, md), (bg, bu, bd)
    flag = swapped[lax.rem(lax.axis_index("expert"), EXPERTS // 2)]

    def go(sources):
        loads, stores = [], []
        for part in range(PIECES):
            for k, (src, buf, dst) in enumerate(zip(sources, bufs, outs)):
                rows = src.shape[1] // PIECES
                at = pl.ds(part * rows, rows)
                loads.append(pltpu.make_async_copy(src.at[0, at], buf.at[at], in_sem.at[k, part]))
                stores.append(pltpu.make_async_copy(buf.at[at], dst.at[0, at], out_sem.at[k, part]))
        for cp in loads:
            cp.start()
        for load, store in zip(loads, stores):
            load.wait()
            store.start()
        for cp in stores:
            cp.wait()

    @pl.when(flag == 1)
    def _():
        go((rg, ru, rd))

    @pl.when(flag != 1)
    def _():
        go((og, ou, od))


def pick(swapped, mixed, own, received):
    any_spec = pl.BlockSpec(memory_space=pl.ANY)
    vmem_spec = pl.BlockSpec(memory_space=pltpu.VMEM)
    return pl.pallas_call(
        pick_kernel,
        out_shape=tuple(jax.ShapeDtypeStruct(a.shape, a.dtype) for a in (mixed, *own)),
        in_specs=[pl.BlockSpec(memory_space=pltpu.SMEM), vmem_spec] + [any_spec] * 6,
        out_specs=(vmem_spec,) + (any_spec,) * 3,
        scratch_shapes=[pltpu.VMEM(a.shape[1:], a.dtype) for a in own]
        + [pltpu.SemaphoreType.DMA((3, PIECES)), pltpu.SemaphoreType.DMA((3, PIECES))],
        compiler_params=pltpu.CompilerParams(vmem_limit_bytes=64 * 1024 * 1024),
        name="pick_slab",
    )(swapped, mixed, *own, *received)


def on_device(tokens, routes, gates, swapped, gate_weight, up_weight, down_weight):
    mixed, got_gate, got_down, number = moe(
        swapped, tokens, routes, gates, gate_weight, up_weight, down_weight
    )
    got_up = lax.switch(
        number[0], [functools.partial(exchange, p) for p in SETS], up_weight
    )
    return pick(
        swapped, mixed, (gate_weight, up_weight, down_weight), (got_gate, got_up, got_down)
    )


def solution(mesh):
    in_specs = (
        P(("expert", "dp"), None),
        P(("expert", "dp"), None),
        P(("expert", "dp"), None),
        P(),
        P("expert", None, "dp"),
        P("expert", None, "dp"),
        P("expert", "dp", None),
    )
    out_specs = (
        P(("expert", "dp"), None),
        P("expert", None, "dp"),
        P("expert", None, "dp"),
        P("expert", "dp", None),
    )
    return jax.shard_map(
        on_device, mesh=mesh, in_specs=in_specs, out_specs=out_specs, check_vma=False
    )
```

```python
import functools

import jax
import jax.numpy as jnp
from jax import lax
from jax.experimental import pallas as pl
from jax.experimental.pallas import tpu as pltpu
from jax.sharding import PartitionSpec as P

D = 7168
FF = 2048
EXPERTS = 16
Q = D // 4
EXT = 128
W0 = Q + EXT
BF = jnp.bfloat16
F32 = jnp.float32
MESH = pl.DeviceIdType.MESH
PIECES = 8
FIRST, SECOND, THIRD, FOURTH = 1, 12, 3, 0

CHUNKS = 10
UNIT = 16
MOVED = CHUNKS * 56 * UNIT
EARLY = 2 * D - MOVED

ROUTES = {
    15: ((1, 29), (0, 27), (11, 29), (10, 27), (21, 29), (20, 27), (31, 29), (30, 27)),
    41: ((1, 22), (0, 20), (3, 7), (5, 7), (29, 13), (31, 23), (30, 20), (43, 23), (42, 13), (45, 20)),
    51: ((1, 29), (7, 27), (11, 29), (13, 27), (33, 29), (39, 27), (43, 29), (45, 27)),
    61: ((1, 36), (3, 20), (19, 13), (21, 36), (20, 7), (31, 36), (30, 20), (33, 36), (37, 7), (39, 13), (43, 36), (45, 20)),
    85: ((1, 29), (3, 27), (21, 29), (23, 27), (33, 29), (35, 27), (53, 29), (55, 27)),
    103: ((1, 36), (0, 20), (8, 6), (11, 37), (15, 13), (21, 36), (23, 20), (41, 6), (43, 37), (47, 13), (53, 36), (55, 20)),
    107: ((1, 36), (0, 20), (11, 36), (13, 20), (29, 13), (31, 36), (30, 7), (41, 13), (43, 36), (47, 7), (53, 36), (55, 20)),
    119: ((1, 43), (7, 13), (11, 43), (15, 13), (21, 43), (23, 13), (33, 43), (39, 13), (43, 43), (47, 13), (53, 43), (55, 13)),
    127: ((1, 50), (6, 6), (11, 50), (14, 6), (21, 50), (22, 6), (31, 50), (30, 6), (33, 50), (39, 6), (43, 50), (47, 6), (53, 50), (55, 6)),
    151: ((1, 36), (7, 20), (11, 36), (10, 20), (21, 36), (20, 20), (33, 36), (35, 13), (37, 7), (61, 7), (63, 36), (62, 13)),
    153: ((1, 29), (3, 27), (29, 27), (31, 29), (33, 29), (35, 27), (61, 27), (63, 29)),
    165: ((1, 29), (3, 27), (21, 29), (23, 27), (43, 29), (45, 27), (57, 27), (63, 29)),
    171: ((1, 36), (0, 20), (8, 6), (11, 37), (13, 13), (29, 20), (31, 36), (41, 6), (43, 37), (45, 13), (61, 20), (63, 36)),
    187: ((1, 43), (5, 13), (11, 43), (13, 13), (29, 13), (31, 43), (33, 43), (37, 13), (43, 43), (45, 13), (61, 13), (63, 43)),
    195: ((1, 29), (0, 27), (11, 29), (13, 27), (51, 27), (53, 29), (63, 29), (62, 27)),
    205: ((1, 36), (0, 20), (19, 20), (21, 36), (24, 6), (27, 13), (31, 37), (51, 20), (53, 36), (57, 6), (59, 13), (63, 37)),
    219: ((1, 43), (5, 13), (11, 43), (10, 13), (29, 13), (31, 43), (33, 43), (35, 13), (53, 43), (52, 13), (59, 13), (63, 43)),
    221: ((1, 43), (3, 13), (19, 13), (21, 43), (27, 13), (31, 43), (33, 43), (35, 13), (51, 13), (53, 43), (59, 13), (63, 43)),
    231: ((1, 43), (7, 13), (11, 43), (15, 13), (21, 43), (23, 13), (41, 13), (43, 43), (49, 13), (53, 43), (57, 13), (63, 43)),
    237: ((1, 43), (3, 13), (19, 13), (21, 43), (27, 13), (31, 43), (41, 13), (43, 43), (49, 13), (53, 43), (57, 13), (63, 43)),
    239: ((1, 50), (0, 6), (8, 6), (11, 50), (16, 6), (21, 50), (24, 6), (31, 50), (41, 6), (43, 50), (49, 6), (53, 50), (57, 6), (63, 50)),
    241: ((1, 36), (3, 6), (7, 14), (33, 37), (34, 7), (36, 12), (43, 36), (42, 20), (53, 36), (52, 20), (63, 36), (62, 20)),
    247: ((1, 50), (7, 6), (11, 50), (15, 6), (21, 50), (23, 6), (33, 50), (38, 6), (43, 50), (46, 6), (53, 50), (54, 6), (63, 50), (62, 6)),
    255: ((1, 56), (11, 56), (21, 56), (31, 56), (33, 56), (43, 56), (53, 56), (63, 56)),
}
SETS = sorted(ROUTES)
SERVES = (
    1, 0, 0, 0, 1, 0, 0, 0, 2, 2, 4, 9, 10, 13, 3, 8,
    1, 2, 11, 5, 1, 12, 3, 8, 2, 2, 3, 7, 3, 13, 3, 8,
    4, 14, 4, 5, 15, 6, 15, 8, 4, 7, 4, 7, 16, 16, 17, 8,
    5, 5, 5, 5, 6, 6, 19, 8, 21, 7, 7, 7, 8, 8, 8, 8,
    10, 14, 11, 9, 10, 12, 15, 20, 10, 9, 9, 9, 10, 13, 17, 23,
    11, 12, 11, 18, 12, 12, 19, 20, 21, 13, 22, 22, 13, 13, 23, 23,
    14, 14, 15, 18, 15, 16, 15, 20, 21, 16, 17, 22, 16, 16, 17, 23,
    21, 18, 18, 18, 19, 20, 19, 20, 21, 22, 22, 22, 23, 23, 23, 23,
)


def legs_of(z, ring, direct, sign):
    stops = [(0, z)]
    if ring != z:
        stops.append((0, ring))
    if not direct:
        stops.append((-sign, ring))
    stops.append((2, z))
    return list(zip(stops[:-1], stops[1:]))


class Leg:
    pass


def layout(pairs):
    lands, relay_rows = {}, {}
    legs = []
    base = {}
    for code, units in ROUTES[pairs]:
        parity, z, ring, direct = code // 32, code // 8 % 4, code // 2 % 4, code % 2
        rows = units * UNIT
        start = base.get((parity, z), 0)
        base[parity, z] = start + rows * CHUNKS
        before = None
        steps = legs_of(z, ring, direct, 1 - 2 * parity)
        for k, (a, b) in enumerate(steps):
            leg = Leg()
            leg.rows, leg.start, leg.before, leg.turn = rows, start, before, k
            leg.final = k == len(steps) - 1
            leg.move = (b[0] - a[0], b[1])
            leg.back = (a[0] - b[0], a[1])
            leg.sender = ((parity + a[0]) % 2, a[1])
            leg.taker = ((parity + b[0]) % 2, b[1])
            if not leg.final:
                leg.land_slot = lands.get(leg.taker, 0)
                lands[leg.taker] = leg.land_slot + 1
                leg.relay = relay_rows.get(leg.taker, 0)
                relay_rows[leg.taker] = leg.relay + rows * CHUNKS
            legs.append(leg)
            before = leg
    return legs, max(lands.values(), default=1), max(relay_rows.values(), default=UNIT)


def exchange_kernel(legs, src, dst, relay, end_sem, land_sem):
    e = lax.axis_index("expert")
    d = lax.axis_index("dp")
    x, z = e // 4, lax.rem(e, 4)

    def device(move):
        return (lax.rem(x + move[0] + 4, 4) * 4 + move[1], d)

    kinds = sorted({leg.sender for leg in legs} | {leg.taker for leg in legs})
    barrier = pltpu.get_barrier_semaphore()
    for kind in kinds:
        @pl.when((lax.rem(x, 2) == kind[0]) & (z == kind[1]))
        def _(kind=kind):
            peers = {(leg.move[0] % 4, leg.move[1]) for leg in legs if leg.sender == kind}
            peers |= {(leg.back[0] % 4, leg.back[1]) for leg in legs if leg.taker == kind}
            for move in sorted(peers):
                pl.semaphore_signal(barrier, inc=1, device_id=device(move), device_id_type=MESH)
            pl.semaphore_wait(barrier, len(peers))

    def own(leg, chunk):
        return pl.ds(pl.multiple_of(leg.start + chunk * leg.rows, UNIT), leg.rows)

    def spot(leg, chunk):
        if leg.final:
            return dst.at[0, own(leg, chunk)]
        return relay.at[pl.ds(pl.multiple_of(leg.relay + chunk * leg.rows, UNIT), leg.rows)]

    def copy(leg, chunk):
        return pltpu.make_async_remote_copy(
            src_ref=src.at[0, own(leg, chunk)] if leg.turn == 0 else spot(leg.before, chunk),
            dst_ref=spot(leg, chunk),
            send_sem=end_sem.at[min(leg.turn, 1)],
            recv_sem=end_sem.at[2] if leg.final else land_sem.at[leg.land_slot, chunk],
            device_id=device(leg.move), device_id_type=MESH,
        )

    def arrival(leg, chunk):
        here = spot(leg, chunk)
        return pltpu.make_async_remote_copy(
            src_ref=here, dst_ref=here,
            send_sem=end_sem.at[0],
            recv_sem=land_sem.at[leg.land_slot, chunk],
            device_id=device((2, z)), device_id_type=MESH,
        )

    def whole(ref):
        return pltpu.make_async_remote_copy(
            src_ref=ref, dst_ref=ref, send_sem=end_sem.at[0], recv_sem=end_sem.at[2],
            device_id=device((2, z)), device_id_type=MESH,
        )

    for kind in kinds:
        @pl.when((lax.rem(x, 2) == kind[0]) & (z == kind[1]))
        def _(kind=kind):
            out = [leg for leg in legs if leg.sender == kind]
            late = max([leg.turn for leg in out], default=0)

            def push(step, carry):
                for turn in range(late + 1):
                    chunk = step - turn

                    @pl.when((chunk >= 0) & (chunk < CHUNKS))
                    def _(turn=turn, chunk=chunk):
                        for leg in out:
                            if leg.turn == turn:
                                if turn:
                                    arrival(leg.before, chunk).wait_recv()
                                copy(leg, chunk).start()
                return carry

            if out:
                lax.fori_loop(0, CHUNKS + late, push, 0)
            passed = sum(leg.rows for leg in out if leg.turn) * CHUNKS
            if any(leg.final and leg.taker == kind for leg in legs):
                whole(dst.at[0]).wait_recv()
                whole(src.at[0]).wait_send()
            if passed:
                relayed = relay.at[pl.ds(0, passed)]
                pltpu.make_async_remote_copy(
                    src_ref=relayed, dst_ref=relayed,
                    send_sem=end_sem.at[1], recv_sem=end_sem.at[2],
                    device_id=device((2, z)), device_id_type=MESH,
                ).wait_send()


def exchange(pairs, weight):
    any_spec = pl.BlockSpec(memory_space=pl.ANY)
    legs, n_land, n_relay = layout(pairs)
    return pl.pallas_call(
        functools.partial(exchange_kernel, legs),
        out_shape=jax.ShapeDtypeStruct(weight.shape, weight.dtype),
        in_specs=[any_spec],
        out_specs=any_spec,
        scratch_shapes=[
            pltpu.VMEM((n_relay, 256), BF),
            pltpu.SemaphoreType.DMA((3,)),
            pltpu.SemaphoreType.DMA((n_land, CHUNKS)),
        ],
        compiler_params=pltpu.CompilerParams(
            collective_id=1 + pairs // 2, has_side_effects=True, vmem_limit_bytes=60 * 1024 * 1024
        ),
        cost_estimate=pl.CostEstimate(flops=0, bytes_accessed=64 * 1024 * 1024, transcendentals=0),
        name="exchange_%d" % pairs,
    )(weight)


def moe_kernel(
    swapped, tok, routes, gates, gw, uw, dw,
    out, rg, rd, rest, number,
    x0, x1, o0, o1, wg, wu, wd,
    mine0, mine1, send0, send1, core0, core1,
    r1a, r1b, s2a, s2b, r2a, r2b, s3a, s3b, r3a, r3b,
    half_to, half_in, half_out, last_in,
    wsem, swap_s, swap_r, core_s, core_r, ag_s, ag_r, fw_s, fw_r, pc_s, pc_r, rs_s, rs_r, last_s, last_r, z_s, z_r,
):
    e = lax.axis_index("expert")
    d = lax.axis_index("dp")
    x, z = e // 4, lax.rem(e, 4)
    y, c = d // 2, lax.rem(d, 2)

    def shift(value, by):
        return lax.rem(value + by, 4)

    def device(px, pz, py, pc):
        return (px * 4 + pz, py * 2 + pc)

    other = device(x, z, y, 1 - c)
    along = {
        "x": lambda i: device(shift(x, i), z, y, c),
        "z": lambda i: device(x, shift(z, i), y, c),
        "y": lambda i: device(x, z, shift(y, i), c),
    }

    def remote(src, dst, ss, rs, dev):
        return pltpu.make_async_remote_copy(
            src_ref=src, dst_ref=dst, send_sem=ss, recv_sem=rs,
            device_id=dev, device_id_type=MESH,
        )

    loads = [
        pltpu.make_async_copy(gw.at[0], wg, wsem.at[0]),
        pltpu.make_async_copy(uw.at[0], wu, wsem.at[1]),
        pltpu.make_async_copy(dw.at[0], wd, wsem.at[2]),
    ]
    for cp in loads:
        cp.start()

    barrier = pltpu.get_barrier_semaphore()
    peers = [other] + [along[a](i) for a in "xzy" for i in (1, 2, 3)]
    for dev in peers:
        pl.semaphore_signal(barrier, inc=1, device_id=dev, device_id_type=MESH)

    wide = tok[...].astype(F32)
    named, level = routes[...], gates[...].astype(F32)
    slot = lax.broadcasted_iota(jnp.int32, (8, EXT), 1)
    by_expert = jnp.zeros((8, EXT), F32)
    for k in range(8):
        by_expert += jnp.where(named[:, k : k + 1] == slot, level[:, k : k + 1], 0.0)
    low, high = wide[:, 0 : 2 * Q], wide[:, 2 * Q :]
    half_to[:, 0 : 2 * Q] = jnp.where(c == 0, high, low)
    half_to[:, 2 * Q :] = by_expert
    own = jnp.concatenate([jnp.where(c == 0, low, high), by_expert], axis=1)
    pl.semaphore_wait(barrier, len(peers))

    def slab_piece(k, part):
        src, dst = ((gw, rg), (dw, rd))[k]
        rows = dst.shape[1] // PIECES
        at = (0, pl.ds(part * rows, rows))
        return remote(src.at[at], dst.at[at], swap_s.at[k, part], swap_r.at[k, part], along["x"](2))

    swaps = [slab_piece(k, part) for k in range(2) for part in range(PIECES)]
    waiting = list(swaps)

    def send_pieces(number):
        for cp in waiting[:number]:
            cp.start()
        del waiting[:number]

    send_pieces(FIRST)

    bits = swapped[1]
    for k in range(2, 8):
        bits += swapped[k] * 2 ** (k - 1)
    serving = jnp.int32(0)
    for n, serves in enumerate(SERVES):
        serving += jnp.where(bits == n, serves, 0)
    number[0] = serving

    first = remote(half_to, half_in, core_s.at[0], core_r.at[0], other)
    first.start()

    first.wait()
    got = half_in[...]
    block = jnp.where(
        c == 0, jnp.concatenate([own, got], axis=0), jnp.concatenate([got, own], axis=0)
    ).astype(BF)
    rows16 = pl.ds(pl.multiple_of(x * 16, 16), 16)
    x0[y, z, rows16, 0:Q] = block[:, 0:Q]
    x0[y, z, rows16, Q:W0] = block[:, 2 * Q : 2 * Q + EXT]
    x1[y, z, rows16, :] = block[:, Q : 2 * Q]

    sent = []

    def gather(stream, stage, i, buf, view, axis):
        cp = remote(
            buf.at[view], buf.at[view], ag_s.at[stream, stage, i - 1], ag_r.at[stream, stage, i - 1],
            along[axis](i),
        )
        cp.start()
        sent.append(cp)

    def landed(stream, stage, i, buf, view):
        remote(
            buf.at[view], buf.at[view], ag_s.at[stream, stage, i - 1], ag_r.at[stream, stage, i - 1], other
        ).wait_recv()

    for i in (1, 2, 3):
        gather(0, 0, i, x0, (y, z, rows16), "x")
        gather(1, 0, i, x1, (y, z, rows16), "x")
    send_pieces(SECOND)

    for i in (1, 2, 3):
        from16 = pl.ds(pl.multiple_of(shift(x, 4 - i) * 16, 16), 16)
        landed(0, 0, i, x0, (y, z, from16))
        landed(1, 0, i, x1, (y, z, from16))

    def block_at(stream, first, second):
        if stream == 0:
            return (shift(y, second), shift(z, first))
        return (shift(y, first), shift(z, second))

    def spread(stream, j):
        buf, axis = ((x0, "y"), (x1, "z"))[stream]
        view = block_at(stream, j, 0)
        for i in (1, 3, 2):
            cp = remote(
                buf.at[view], buf.at[view],
                last_s.at[stream, i - 1, j], last_r.at[stream, i - 1, j], along[axis](i),
            )
            cp.start()
            sent.append(cp)

    for i in (1, 3, 2):
        gather(0, 1, i, x0, (y, z), "z")
        gather(1, 1, i, x1, (y, z), "y")
    spread(0, 0)
    spread(1, 0)
    for i in (1, 3, 2):
        landed(0, 1, i, x0, block_at(0, 4 - i, 0))
        spread(0, 4 - i)
        landed(1, 1, i, x1, block_at(1, 4 - i, 0))
        spread(1, 4 - i)

    every = slice(None)
    forwards = []

    def forward(stream, i, view):
        src, dst = ((x0, o0), (x1, o1))[stream]
        cp = remote(src.at[view], dst.at[view], fw_s.at[stream, i], fw_r.at[stream, i], other)
        cp.start()
        forwards.append(cp)

    forward(0, 0, (y,))
    forward(1, 0, (every, z))
    for i in (1, 3, 2):
        for stream, buf in ((0, x0), (1, x1)):
            for j in range(4):
                view = block_at(stream, j, 4 - i)
                remote(
                    buf.at[view], buf.at[view],
                    last_s.at[stream, i - 1, j], last_r.at[stream, i - 1, j], other,
                ).wait_recv()
        forward(0, i, (shift(y, 4 - i),))
        forward(1, i, (every, shift(z, 4 - i)))
    for cp in forwards:
        cp.wait()
    for cp in sent:
        cp.wait_send()
    for cp in loads:
        cp.wait()

    stores = [
        pltpu.make_async_copy(wu, rest.at[0, pl.ds(0, D)], wsem.at[0]),
        pltpu.make_async_copy(wg.at[pl.ds(EARLY, D - EARLY)], rest.at[0, pl.ds(D, D - EARLY)], wsem.at[1]),
    ]
    for cp in stores:
        cp.start()

    lane = lax.broadcasted_iota(jnp.int32, (128, EXT), 1)
    lo = pl.multiple_of(c * 2 * Q, 2 * Q)
    hi = pl.multiple_of((1 - c) * 2 * Q, 2 * Q)

    def rows_of(ref, a, b):
        return ref[a, pl.ds(b * 2, 2)].reshape(128, ref.shape[-1])

    def turn(t, carry):
        a, b = t // 2, lax.rem(t, 2)
        full = rows_of(x0, a, b)
        parts = (
            (full[:, 0:Q], lo),
            (rows_of(x1, a, b), lo + Q),
            (rows_of(o0, a, b)[:, 0:Q], hi),
            (rows_of(o1, a, b), hi + Q),
        )
        gate = jnp.zeros((128, 256), F32)
        up = jnp.zeros((128, 256), F32)
        for part, start in parts:
            at = pl.ds(pl.multiple_of(start, Q), Q)
            gate += jnp.dot(part, wg[at, :], preferred_element_type=F32)
            up += jnp.dot(part, wu[at, :], preferred_element_type=F32)
        gate = gate * D ** (-0.5)
        up = up * D ** (-0.5)
        hidden = (gate / (1.0 + jnp.exp(-gate)) * up).astype(BF)
        weight = jnp.sum(
            jnp.where(lane == e, full[:, Q:W0].astype(F32), 0.0), axis=1, keepdims=True
        ) * FF ** (-0.5)
        for dst, start in ((send0, hi), (send1, hi + Q), (mine0, lo), (mine1, lo + Q)):
            at = pl.ds(pl.multiple_of(start, Q), Q)
            value = jnp.dot(hidden, wd[:, at], preferred_element_type=F32) * weight
            dst[a, pl.ds(b * 2, 2)] = value.astype(BF).reshape(2, 64, Q)
        return carry

    def part_copy(stream, a):
        src, dst = ((send0, core0), (send1, core1))[stream]
        return remote(src.at[a], dst.at[a], pc_s.at[stream, a], pc_r.at[stream, a], other)

    out_copies = []

    def scatter(stream, stage, i, src, dst, axis):
        cp = remote(src, dst, rs_s.at[stream, stage, i - 1], rs_r.at[stream, stage, i - 1], along[axis](i))
        cp.start()
        out_copies.append(cp)
        return cp

    def total(own_value, got_ref, at=()):
        value = own_value.astype(F32)
        for i in range(3):
            value += got_ref[(i,) + at].astype(F32)
        return value

    def first_y(p):
        return remote(
            mine0.at[shift(y, p + 1)], r1a.at[p], rs_s.at[0, 0, p], rs_r.at[0, 0, p], along["y"](p + 1)
        )

    def first_z(p, i):
        a = shift(y, p + 1)
        return remote(
            mine1.at[a, shift(z, i)], r1b.at[i - 1, a], z_s.at[i - 1, p], z_r.at[i - 1, p], along["z"](i)
        )

    def quarter(q, carry):
        @pl.when(q < 4)
        def _():
            a = shift(y, q + 1)
            lax.fori_loop(2 * a, 2 * a + 2, turn, 0)
            part_copy(0, a).start()
            part_copy(1, a).start()

        @pl.when(q > 0)
        def _():
            p = q - 1
            a = shift(y, p + 1)
            part_copy(0, a).wait()
            part_copy(1, a).wait()
            for own_ref, got_ref in ((mine0, core0), (mine1, core1)):
                for b in range(4):
                    own_ref[a, b] = (own_ref[a, b].astype(F32) + got_ref[a, b].astype(F32)).astype(BF)
            for i in (1, 3, 2):
                first_z(p, i).start()

            @pl.when(p < 3)
            def _():
                first_y(p).start()

        return carry

    lax.fori_loop(0, 5, quarter, 0)
    send_pieces(THIRD)

    def first_landed(p, carry):
        for i in (1, 2, 3):
            first_z(p, i).wait()
        return carry

    lax.fori_loop(0, 4, first_landed, 0)
    for p in range(3):
        first_y(p).wait()
    for b in range(4):
        s2a[b] = total(mine0[y, b], r1a, (b,)).astype(BF)
        s2b[b] = total(mine1[b, z], r1b, (b,)).astype(BF)
    stage = []
    for i in (1, 2, 3):
        stage.append(scatter(0, 1, i, s2a.at[shift(z, i)], r2a.at[i - 1], "z"))
        stage.append(scatter(1, 1, i, s2b.at[shift(y, i)], r2b.at[i - 1], "y"))
    send_pieces(FOURTH)
    for cp in stage:
        cp.wait_recv()
    s3a[...] = total(s2a[z], r2a).astype(BF)
    s3b[...] = total(s2b[y], r2b).astype(BF)
    stage = []
    for i in (1, 2, 3):
        to16 = pl.ds(pl.multiple_of(shift(x, i) * 16, 16), 16)
        stage.append(scatter(0, 2, i, s3a.at[to16], r3a.at[i - 1], "x"))
        stage.append(scatter(1, 2, i, s3b.at[to16], r3b.at[i - 1], "x"))
    send_pieces(len(waiting))
    for cp in stage:
        cp.wait_recv()
    sum_a = total(s3a[rows16, :], r3a)
    sum_b = total(s3b[rows16, :], r3b)
    keep_a = jnp.where(c == 0, sum_a[0:8], sum_a[8:16])
    keep_b = jnp.where(c == 0, sum_b[0:8], sum_b[8:16])
    half_out[:, 0:Q] = jnp.where(c == 0, sum_a[8:16], sum_a[0:8])
    half_out[:, Q : 2 * Q] = jnp.where(c == 0, sum_b[8:16], sum_b[0:8])
    last = remote(half_out, last_in, core_s.at[1], core_r.at[1], other)
    last.start()
    last.wait()
    kept = jnp.concatenate([keep_a, keep_b], axis=1)
    given = last_in[...]
    out[:, 0 : 2 * Q] = jnp.where(c == 0, kept, given).astype(BF)
    out[:, 2 * Q :] = jnp.where(c == 0, given, kept).astype(BF)

    for cp in out_copies:
        cp.wait_send()
    for cp in swaps:
        cp.wait()
    for cp in stores:
        cp.wait()


def moe(swapped, tok, routes, gates, gate_weight, up_weight, down_weight):
    vm = lambda *shape: pltpu.VMEM(shape, BF)
    dma = lambda *shape: pltpu.SemaphoreType.DMA(shape)
    any_spec = pl.BlockSpec(memory_space=pl.ANY)
    vmem_spec = pl.BlockSpec(memory_space=pltpu.VMEM)
    smem_spec = pl.BlockSpec(memory_space=pltpu.SMEM)
    like = lambda a: jax.ShapeDtypeStruct(a.shape, a.dtype)
    return pl.pallas_call(
        moe_kernel,
        out_shape=(
            jax.ShapeDtypeStruct((8, D), BF),
            jax.ShapeDtypeStruct((1, EARLY, 256), BF), like(down_weight),
            jax.ShapeDtypeStruct((1, MOVED, 256), BF),
            jax.ShapeDtypeStruct((1,), jnp.int32),
        ),
        in_specs=[smem_spec] + [vmem_spec] * 3 + [any_spec] * 3,
        out_specs=(vmem_spec, any_spec, any_spec, any_spec, smem_spec),
        scratch_shapes=[
            vm(4, 4, 64, W0), vm(4, 4, 64, Q), vm(4, 4, 64, W0), vm(4, 4, 64, Q),
            vm(D, 256), vm(D, 256), vm(256, D),
            vm(4, 4, 64, Q), vm(4, 4, 64, Q), vm(4, 4, 64, Q), vm(4, 4, 64, Q),
            vm(4, 4, 64, Q), vm(4, 4, 64, Q),
            vm(3, 4, 64, Q), vm(3, 4, 64, Q), vm(4, 64, Q), vm(4, 64, Q),
            vm(3, 64, Q), vm(3, 64, Q), vm(64, Q), vm(64, Q), vm(3, 16, Q), vm(3, 16, Q),
            pltpu.VMEM((8, 2 * Q + EXT), F32), pltpu.VMEM((8, 2 * Q + EXT), F32),
            pltpu.VMEM((8, 2 * Q), F32), pltpu.VMEM((8, 2 * Q), F32),
            dma(3), dma(2, PIECES), dma(2, PIECES), dma(2), dma(2),
            dma(2, 3, 3), dma(2, 3, 3), dma(2, 4), dma(2, 4), dma(2, 4), dma(2, 4),
            dma(2, 3, 3), dma(2, 3, 3),
            dma(2, 3, 4), dma(2, 3, 4), dma(3, 4), dma(3, 4),
        ],
        compiler_params=pltpu.CompilerParams(
            collective_id=0, has_side_effects=True, vmem_limit_bytes=64 * 1024 * 1024
        ),
        cost_estimate=pl.CostEstimate(
            flops=6 * 1024 * D * 256, bytes_accessed=33 * 1024 * 1024, transcendentals=1024 * 256
        ),
        name="moe_and_exchange",
    )(swapped, tok, routes, gates, gate_weight, up_weight, down_weight)


def pick_kernel(swapped, mixed, og, ou, od, rg, rx, rd, out, mg, mu, md, bg, bu, bd, in_sem, out_sem):
    out[...] = mixed[...]
    outs, bufs = (mg, mu, md), (bg, bu, bd)
    flag = swapped[lax.rem(lax.axis_index("expert"), EXPERTS // 2)]

    def own(k, start, rows):
        return (og, ou, od)[k].at[0, pl.ds(start, rows)]

    def received(k, start, rows):
        if k == 0 and start < EARLY:
            return rg.at[0, pl.ds(start, rows)]
        if k < 2:
            return rx.at[0, pl.ds(start if k else D + start - EARLY, rows)]
        return rd.at[0, pl.ds(start, rows)]

    def go(source):
        loads, stores = [], []
        for part in range(PIECES):
            for k, (buf, dst) in enumerate(zip(bufs, outs)):
                rows = dst.shape[1] // PIECES
                at = pl.ds(part * rows, rows)
                loads.append(
                    pltpu.make_async_copy(source(k, part * rows, rows), buf.at[at], in_sem.at[k, part])
                )
                stores.append(pltpu.make_async_copy(buf.at[at], dst.at[0, at], out_sem.at[k, part]))
        for cp in loads:
            cp.start()
        for load, store in zip(loads, stores):
            load.wait()
            store.start()
        for cp in stores:
            cp.wait()

    @pl.when(flag == 1)
    def _():
        go(received)

    @pl.when(flag != 1)
    def _():
        go(own)


def pick(swapped, mixed, own, received):
    any_spec = pl.BlockSpec(memory_space=pl.ANY)
    vmem_spec = pl.BlockSpec(memory_space=pltpu.VMEM)
    return pl.pallas_call(
        pick_kernel,
        out_shape=tuple(jax.ShapeDtypeStruct(a.shape, a.dtype) for a in (mixed, *own)),
        in_specs=[pl.BlockSpec(memory_space=pltpu.SMEM), vmem_spec] + [any_spec] * 6,
        out_specs=(vmem_spec,) + (any_spec,) * 3,
        scratch_shapes=[pltpu.VMEM(a.shape[1:], a.dtype) for a in own]
        + [pltpu.SemaphoreType.DMA((3, PIECES)), pltpu.SemaphoreType.DMA((3, PIECES))],
        compiler_params=pltpu.CompilerParams(vmem_limit_bytes=64 * 1024 * 1024),
        name="pick_slab",
    )(swapped, mixed, *own, *received)


def on_device(tokens, routes, gates, swapped, gate_weight, up_weight, down_weight):
    mixed, got_gate, got_down, rest, number = moe(
        swapped, tokens, routes, gates, gate_weight, up_weight, down_weight
    )
    got_rest = lax.switch(number[0], [functools.partial(exchange, p) for p in SETS], rest)
    return pick(
        swapped, mixed, (gate_weight, up_weight, down_weight), (got_gate, got_rest, got_down)
    )


def solution(mesh):
    in_specs = (
        P(("expert", "dp"), None),
        P(("expert", "dp"), None),
        P(("expert", "dp"), None),
        P(),
        P("expert", None, "dp"),
        P("expert", None, "dp"),
        P("expert", "dp", None),
    )
    out_specs = (
        P(("expert", "dp"), None),
        P("expert", None, "dp"),
        P("expert", None, "dp"),
        P("expert", "dp", None),
    )
    return jax.shard_map(
        on_device, mesh=mesh, in_specs=in_specs, out_specs=out_specs, check_vma=False
    )
```

```python
import functools

import jax
import jax.numpy as jnp
from jax import lax
from jax.experimental import pallas as pl
from jax.experimental.pallas import tpu as pltpu
from jax.sharding import PartitionSpec as P

D = 7168
FF = 2048
EXPERTS = 16
Q = D // 4
EXT = 128
W0 = Q + EXT
BF = jnp.bfloat16
F32 = jnp.float32
MESH = pl.DeviceIdType.MESH
PIECES = 8
FIRST, SECOND, THIRD, FOURTH = 2, 13, 1, 0

CHUNKS = 10
UNIT = 16
MOVED = CHUNKS * 56 * UNIT
EARLY = 2 * D - MOVED

ROUTES = {
    15: ((1, 29), (0, 27), (11, 29), (10, 27), (21, 29), (20, 27), (31, 29), (30, 27)),
    41: ((1, 22), (0, 20), (3, 7), (5, 7), (29, 13), (31, 23), (30, 20), (43, 23), (42, 13), (45, 20)),
    51: ((1, 29), (7, 27), (11, 29), (13, 27), (33, 29), (39, 27), (43, 29), (45, 27)),
    61: ((1, 36), (3, 20), (19, 13), (21, 36), (20, 7), (31, 36), (30, 20), (33, 36), (37, 7), (39, 13), (43, 36), (45, 20)),
    85: ((1, 29), (3, 27), (21, 29), (23, 27), (33, 29), (35, 27), (53, 29), (55, 27)),
    103: ((1, 36), (0, 20), (8, 6), (11, 37), (15, 13), (21, 36), (23, 20), (41, 6), (43, 37), (47, 13), (53, 36), (55, 20)),
    107: ((1, 36), (0, 20), (11, 36), (13, 20), (29, 13), (31, 36), (30, 7), (41, 13), (43, 36), (47, 7), (53, 36), (55, 20)),
    119: ((1, 43), (7, 13), (11, 43), (15, 13), (21, 43), (23, 13), (33, 43), (39, 13), (43, 43), (47, 13), (53, 43), (55, 13)),
    127: ((1, 50), (6, 6), (11, 50), (14, 6), (21, 50), (22, 6), (31, 50), (30, 6), (33, 50), (39, 6), (43, 50), (47, 6), (53, 50), (55, 6)),
    151: ((1, 36), (7, 20), (11, 36), (10, 20), (21, 36), (20, 20), (33, 36), (35, 13), (37, 7), (61, 7), (63, 36), (62, 13)),
    153: ((1, 29), (3, 27), (29, 27), (31, 29), (33, 29), (35, 27), (61, 27), (63, 29)),
    165: ((1, 29), (3, 27), (21, 29), (23, 27), (43, 29), (45, 27), (57, 27), (63, 29)),
    171: ((1, 36), (0, 20), (8, 6), (11, 37), (13, 13), (29, 20), (31, 36), (41, 6), (43, 37), (45, 13), (61, 20), (63, 36)),
    187: ((1, 43), (5, 13), (11, 43), (13, 13), (29, 13), (31, 43), (33, 43), (37, 13), (43, 43), (45, 13), (61, 13), (63, 43)),
    195: ((1, 29), (0, 27), (11, 29), (13, 27), (51, 27), (53, 29), (63, 29), (62, 27)),
    205: ((1, 36), (0, 20), (19, 20), (21, 36), (24, 6), (27, 13), (31, 37), (51, 20), (53, 36), (57, 6), (59, 13), (63, 37)),
    219: ((1, 43), (5, 13), (11, 43), (10, 13), (29, 13), (31, 43), (33, 43), (35, 13), (53, 43), (52, 13), (59, 13), (63, 43)),
    221: ((1, 43), (3, 13), (19, 13), (21, 43), (27, 13), (31, 43), (33, 43), (35, 13), (51, 13), (53, 43), (59, 13), (63, 43)),
    231: ((1, 43), (7, 13), (11, 43), (15, 13), (21, 43), (23, 13), (41, 13), (43, 43), (49, 13), (53, 43), (57, 13), (63, 43)),
    237: ((1, 43), (3, 13), (19, 13), (21, 43), (27, 13), (31, 43), (41, 13), (43, 43), (49, 13), (53, 43), (57, 13), (63, 43)),
    239: ((1, 50), (0, 6), (8, 6), (11, 50), (16, 6), (21, 50), (24, 6), (31, 50), (41, 6), (43, 50), (49, 6), (53, 50), (57, 6), (63, 50)),
    241: ((1, 36), (3, 6), (7, 14), (33, 37), (34, 7), (36, 12), (43, 36), (42, 20), (53, 36), (52, 20), (63, 36), (62, 20)),
    247: ((1, 50), (7, 6), (11, 50), (15, 6), (21, 50), (23, 6), (33, 50), (38, 6), (43, 50), (46, 6), (53, 50), (54, 6), (63, 50), (62, 6)),
    255: ((1, 56), (11, 56), (21, 56), (31, 56), (33, 56), (43, 56), (53, 56), (63, 56)),
}
SETS = sorted(ROUTES)
SERVES = (
    1, 0, 0, 0, 1, 0, 0, 0, 2, 2, 4, 9, 10, 13, 3, 8,
    1, 2, 11, 5, 1, 12, 3, 8, 2, 2, 3, 7, 3, 13, 3, 8,
    4, 14, 4, 5, 15, 6, 15, 8, 4, 7, 4, 7, 16, 16, 17, 8,
    5, 5, 5, 5, 6, 6, 19, 8, 21, 7, 7, 7, 8, 8, 8, 8,
    10, 14, 11, 9, 10, 12, 15, 20, 10, 9, 9, 9, 10, 13, 17, 23,
    11, 12, 11, 18, 12, 12, 19, 20, 21, 13, 22, 22, 13, 13, 23, 23,
    14, 14, 15, 18, 15, 16, 15, 20, 21, 16, 17, 22, 16, 16, 17, 23,
    21, 18, 18, 18, 19, 20, 19, 20, 21, 22, 22, 22, 23, 23, 23, 23,
)


def legs_of(z, ring, direct, sign):
    stops = [(0, z)]
    if ring != z:
        stops.append((0, ring))
    if not direct:
        stops.append((-sign, ring))
    stops.append((2, z))
    return list(zip(stops[:-1], stops[1:]))


class Leg:
    pass


def layout(pairs):
    lands, relay_rows = {}, {}
    legs = []
    base = {}
    for code, units in ROUTES[pairs]:
        parity, z, ring, direct = code // 32, code // 8 % 4, code // 2 % 4, code % 2
        rows = units * UNIT
        start = base.get((parity, z), 0)
        base[parity, z] = start + rows * CHUNKS
        before = None
        steps = legs_of(z, ring, direct, 1 - 2 * parity)
        for k, (a, b) in enumerate(steps):
            leg = Leg()
            leg.rows, leg.start, leg.before, leg.turn = rows, start, before, k
            leg.final = k == len(steps) - 1
            leg.move = (b[0] - a[0], b[1])
            leg.back = (a[0] - b[0], a[1])
            leg.sender = ((parity + a[0]) % 2, a[1])
            leg.taker = ((parity + b[0]) % 2, b[1])
            if not leg.final:
                leg.land_slot = lands.get(leg.taker, 0)
                lands[leg.taker] = leg.land_slot + 1
                leg.relay = relay_rows.get(leg.taker, 0)
                relay_rows[leg.taker] = leg.relay + rows * CHUNKS
            legs.append(leg)
            before = leg
    return legs, max(lands.values(), default=1), max(relay_rows.values(), default=UNIT)


def exchange_kernel(legs, src, dst, relay, end_sem, land_sem):
    e = lax.axis_index("expert")
    d = lax.axis_index("dp")
    x, z = e // 4, lax.rem(e, 4)

    def device(move):
        return (lax.rem(x + move[0] + 4, 4) * 4 + move[1], d)

    kinds = sorted({leg.sender for leg in legs} | {leg.taker for leg in legs})
    barrier = pltpu.get_barrier_semaphore()
    for kind in kinds:
        @pl.when((lax.rem(x, 2) == kind[0]) & (z == kind[1]))
        def _(kind=kind):
            peers = {(leg.move[0] % 4, leg.move[1]) for leg in legs if leg.sender == kind}
            peers |= {(leg.back[0] % 4, leg.back[1]) for leg in legs if leg.taker == kind}
            for move in sorted(peers):
                pl.semaphore_signal(barrier, inc=1, device_id=device(move), device_id_type=MESH)
            pl.semaphore_wait(barrier, len(peers))

    def own(leg, chunk):
        return pl.ds(pl.multiple_of(leg.start + chunk * leg.rows, UNIT), leg.rows)

    def spot(leg, chunk):
        if leg.final:
            return dst.at[0, own(leg, chunk)]
        return relay.at[pl.ds(pl.multiple_of(leg.relay + chunk * leg.rows, UNIT), leg.rows)]

    def copy(leg, chunk):
        return pltpu.make_async_remote_copy(
            src_ref=src.at[0, own(leg, chunk)] if leg.turn == 0 else spot(leg.before, chunk),
            dst_ref=spot(leg, chunk),
            send_sem=end_sem.at[min(leg.turn, 1)],
            recv_sem=end_sem.at[2] if leg.final else land_sem.at[leg.land_slot, chunk],
            device_id=device(leg.move), device_id_type=MESH,
        )

    def arrival(leg, chunk):
        here = spot(leg, chunk)
        return pltpu.make_async_remote_copy(
            src_ref=here, dst_ref=here,
            send_sem=end_sem.at[0],
            recv_sem=land_sem.at[leg.land_slot, chunk],
            device_id=device((2, z)), device_id_type=MESH,
        )

    def whole(ref):
        return pltpu.make_async_remote_copy(
            src_ref=ref, dst_ref=ref, send_sem=end_sem.at[0], recv_sem=end_sem.at[2],
            device_id=device((2, z)), device_id_type=MESH,
        )

    for kind in kinds:
        @pl.when((lax.rem(x, 2) == kind[0]) & (z == kind[1]))
        def _(kind=kind):
            out = [leg for leg in legs if leg.sender == kind]
            late = max([leg.turn for leg in out], default=0)

            def push(step, carry):
                for turn in range(late + 1):
                    chunk = step - turn

                    @pl.when((chunk >= 0) & (chunk < CHUNKS))
                    def _(turn=turn, chunk=chunk):
                        for leg in out:
                            if leg.turn == turn:
                                if turn:
                                    arrival(leg.before, chunk).wait_recv()
                                copy(leg, chunk).start()
                return carry

            if out:
                lax.fori_loop(0, CHUNKS + late, push, 0)
            passed = sum(leg.rows for leg in out if leg.turn) * CHUNKS
            if any(leg.final and leg.taker == kind for leg in legs):
                whole(dst.at[0]).wait_recv()
                whole(src.at[0]).wait_send()
            if passed:
                relayed = relay.at[pl.ds(0, passed)]
                pltpu.make_async_remote_copy(
                    src_ref=relayed, dst_ref=relayed,
                    send_sem=end_sem.at[1], recv_sem=end_sem.at[2],
                    device_id=device((2, z)), device_id_type=MESH,
                ).wait_send()


def exchange(pairs, weight):
    any_spec = pl.BlockSpec(memory_space=pl.ANY)
    legs, n_land, n_relay = layout(pairs)
    return pl.pallas_call(
        functools.partial(exchange_kernel, legs),
        out_shape=jax.ShapeDtypeStruct(weight.shape, weight.dtype),
        in_specs=[any_spec],
        out_specs=any_spec,
        scratch_shapes=[
            pltpu.VMEM((n_relay, 256), BF),
            pltpu.SemaphoreType.DMA((3,)),
            pltpu.SemaphoreType.DMA((n_land, CHUNKS)),
        ],
        compiler_params=pltpu.CompilerParams(
            collective_id=1 + pairs // 2, has_side_effects=True, vmem_limit_bytes=60 * 1024 * 1024
        ),
        cost_estimate=pl.CostEstimate(flops=0, bytes_accessed=64 * 1024 * 1024, transcendentals=0),
        name="exchange_%d" % pairs,
    )(weight)


def moe_kernel(
    swapped, tok, routes, gates, gw, uw, dw,
    out, rg, rd, rest, number,
    x0, x1, o0, o1, wg, wu, wd,
    mine0, mine1, send0, send1, core0, core1,
    r1a, r1b, s2a, s2b, r2a, r2b, s3a, s3b, r3a, r3b,
    half_to, half_in, half_out, last_in,
    wsem, swap_s, swap_r, core_s, core_r, ag_s, ag_r, fw_s, fw_r, pc_s, pc_r, rs_s, rs_r, last_s, last_r, z_s, z_r,
):
    e = lax.axis_index("expert")
    d = lax.axis_index("dp")
    x, z = e // 4, lax.rem(e, 4)
    y, c = d // 2, lax.rem(d, 2)

    def shift(value, by):
        return lax.rem(value + by, 4)

    def device(px, pz, py, pc):
        return (px * 4 + pz, py * 2 + pc)

    other = device(x, z, y, 1 - c)
    along = {
        "x": lambda i: device(shift(x, i), z, y, c),
        "z": lambda i: device(x, shift(z, i), y, c),
        "y": lambda i: device(x, z, shift(y, i), c),
    }

    def remote(src, dst, ss, rs, dev):
        return pltpu.make_async_remote_copy(
            src_ref=src, dst_ref=dst, send_sem=ss, recv_sem=rs,
            device_id=dev, device_id_type=MESH,
        )

    loads = [
        pltpu.make_async_copy(gw.at[0], wg, wsem.at[0]),
        pltpu.make_async_copy(uw.at[0], wu, wsem.at[1]),
        pltpu.make_async_copy(dw.at[0], wd, wsem.at[2]),
    ]
    for cp in loads:
        cp.start()

    barrier = pltpu.get_barrier_semaphore()
    peers = [other] + [along[a](i) for a in "xzy" for i in (1, 2, 3)]
    for dev in peers:
        pl.semaphore_signal(barrier, inc=1, device_id=dev, device_id_type=MESH)

    wide = tok[...].astype(F32)
    named, level = routes[...], gates[...].astype(F32)
    slot = lax.broadcasted_iota(jnp.int32, (8, EXT), 1)
    by_expert = jnp.zeros((8, EXT), F32)
    for k in range(8):
        by_expert += jnp.where(named[:, k : k + 1] == slot, level[:, k : k + 1], 0.0)
    low, high = wide[:, 0 : 2 * Q], wide[:, 2 * Q :]
    half_to[:, 0 : 2 * Q] = jnp.where(c == 0, high, low)
    half_to[:, 2 * Q :] = by_expert
    own = jnp.concatenate([jnp.where(c == 0, low, high), by_expert], axis=1)
    pl.semaphore_wait(barrier, len(peers))

    def slab_piece(k, part):
        src, dst = ((gw, rg), (dw, rd))[k]
        rows = dst.shape[1] // PIECES
        at = (0, pl.ds(part * rows, rows))
        return remote(src.at[at], dst.at[at], swap_s.at[k, part], swap_r.at[k, part], along["x"](2))

    swaps = [slab_piece(k, part) for k in range(2) for part in range(PIECES)]
    waiting = list(swaps)

    def send_pieces(number):
        for cp in waiting[:number]:
            cp.start()
        del waiting[:number]

    send_pieces(FIRST)

    bits = swapped[1]
    for k in range(2, 8):
        bits += swapped[k] * 2 ** (k - 1)
    serving = jnp.int32(0)
    for n, serves in enumerate(SERVES):
        serving += jnp.where(bits == n, serves, 0)
    number[0] = serving

    first = remote(half_to, half_in, core_s.at[0], core_r.at[0], other)
    first.start()

    first.wait()
    got = half_in[...]
    block = jnp.where(
        c == 0, jnp.concatenate([own, got], axis=0), jnp.concatenate([got, own], axis=0)
    ).astype(BF)
    rows16 = pl.ds(pl.multiple_of(x * 16, 16), 16)
    x0[y, z, rows16, 0:Q] = block[:, 0:Q]
    x0[y, z, rows16, Q:W0] = block[:, 2 * Q : 2 * Q + EXT]
    x1[y, z, rows16, :] = block[:, Q : 2 * Q]

    sent = []

    def gather(stream, stage, i, buf, view, axis):
        cp = remote(
            buf.at[view], buf.at[view], ag_s.at[stream, stage, i - 1], ag_r.at[stream, stage, i - 1],
            along[axis](i),
        )
        cp.start()
        sent.append(cp)

    def landed(stream, stage, i, buf, view):
        remote(
            buf.at[view], buf.at[view], ag_s.at[stream, stage, i - 1], ag_r.at[stream, stage, i - 1], other
        ).wait_recv()

    for i in (1, 2, 3):
        gather(0, 0, i, x0, (y, z, rows16), "x")
        gather(1, 0, i, x1, (y, z, rows16), "x")
    send_pieces(SECOND)

    for i in (1, 2, 3):
        from16 = pl.ds(pl.multiple_of(shift(x, 4 - i) * 16, 16), 16)
        landed(0, 0, i, x0, (y, z, from16))
        landed(1, 0, i, x1, (y, z, from16))

    def block_at(stream, first, second):
        if stream == 0:
            return (shift(y, second), shift(z, first))
        return (shift(y, first), shift(z, second))

    def spread(stream, j):
        buf, axis = ((x0, "y"), (x1, "z"))[stream]
        view = block_at(stream, j, 0)
        for i in (1, 3, 2):
            cp = remote(
                buf.at[view], buf.at[view],
                last_s.at[stream, i - 1, j], last_r.at[stream, i - 1, j], along[axis](i),
            )
            cp.start()
            sent.append(cp)

    for i in (1, 3, 2):
        gather(0, 1, i, x0, (y, z), "z")
        gather(1, 1, i, x1, (y, z), "y")
    spread(0, 0)
    spread(1, 0)
    for i in (1, 3, 2):
        landed(0, 1, i, x0, block_at(0, 4 - i, 0))
        spread(0, 4 - i)
        landed(1, 1, i, x1, block_at(1, 4 - i, 0))
        spread(1, 4 - i)

    every = slice(None)
    forwards = []

    def forward(stream, i, view):
        src, dst = ((x0, o0), (x1, o1))[stream]
        cp = remote(src.at[view], dst.at[view], fw_s.at[stream, i], fw_r.at[stream, i], other)
        cp.start()
        forwards.append(cp)

    forward(0, 0, (y,))
    forward(1, 0, (every, z))
    for i in (1, 3, 2):
        for stream, buf in ((0, x0), (1, x1)):
            for j in range(4):
                view = block_at(stream, j, 4 - i)
                remote(
                    buf.at[view], buf.at[view],
                    last_s.at[stream, i - 1, j], last_r.at[stream, i - 1, j], other,
                ).wait_recv()
        forward(0, i, (shift(y, 4 - i),))
        forward(1, i, (every, shift(z, 4 - i)))
    for cp in forwards:
        cp.wait()
    for cp in sent:
        cp.wait_send()
    for cp in loads:
        cp.wait()

    stores = [
        pltpu.make_async_copy(wu, rest.at[0, pl.ds(0, D)], wsem.at[0]),
        pltpu.make_async_copy(wg.at[pl.ds(EARLY, D - EARLY)], rest.at[0, pl.ds(D, D - EARLY)], wsem.at[1]),
    ]
    for cp in stores:
        cp.start()

    lane = lax.broadcasted_iota(jnp.int32, (128, EXT), 1)
    lo = pl.multiple_of(c * 2 * Q, 2 * Q)
    hi = pl.multiple_of((1 - c) * 2 * Q, 2 * Q)

    def rows_of(ref, a, b):
        return ref[a, pl.ds(b * 2, 2)].reshape(128, ref.shape[-1])

    def turn(t, carry):
        a, b = t // 2, lax.rem(t, 2)
        full = rows_of(x0, a, b)
        parts = (
            (full[:, 0:Q], lo),
            (rows_of(x1, a, b), lo + Q),
            (rows_of(o0, a, b)[:, 0:Q], hi),
            (rows_of(o1, a, b), hi + Q),
        )
        gate = jnp.zeros((128, 256), F32)
        up = jnp.zeros((128, 256), F32)
        for part, start in parts:
            at = pl.ds(pl.multiple_of(start, Q), Q)
            gate += jnp.dot(part, wg[at, :], preferred_element_type=F32)
            up += jnp.dot(part, wu[at, :], preferred_element_type=F32)
        gate = gate * D ** (-0.5)
        up = up * D ** (-0.5)
        hidden = (gate / (1.0 + jnp.exp(-gate)) * up).astype(BF)
        weight = jnp.sum(
            jnp.where(lane == e, full[:, Q:W0].astype(F32), 0.0), axis=1, keepdims=True
        ) * FF ** (-0.5)
        for dst, start in ((send0, hi), (send1, hi + Q), (mine0, lo), (mine1, lo + Q)):
            at = pl.ds(pl.multiple_of(start, Q), Q)
            value = jnp.dot(hidden, wd[:, at], preferred_element_type=F32) * weight
            dst[a, pl.ds(b * 2, 2)] = value.astype(BF).reshape(2, 64, Q)
        return carry

    def part_copy(stream, a):
        src, dst = ((send0, core0), (send1, core1))[stream]
        return remote(src.at[a], dst.at[a], pc_s.at[stream, a], pc_r.at[stream, a], other)

    out_copies = []

    def scatter(stream, stage, i, src, dst, axis):
        cp = remote(src, dst, rs_s.at[stream, stage, i - 1], rs_r.at[stream, stage, i - 1], along[axis](i))
        cp.start()
        out_copies.append(cp)
        return cp

    def total(own_value, got_ref, at=()):
        value = own_value.astype(F32)
        for i in range(3):
            value += got_ref[(i,) + at].astype(F32)
        return value

    def first_y(p):
        return remote(
            mine0.at[shift(y, p + 1)], r1a.at[p], rs_s.at[0, 0, p], rs_r.at[0, 0, p], along["y"](p + 1)
        )

    def first_z(p, i):
        a = shift(y, p + 1)
        return remote(
            mine1.at[a, shift(z, i)], r1b.at[i - 1, a], z_s.at[i - 1, p], z_r.at[i - 1, p], along["z"](i)
        )

    def quarter(q, carry):
        @pl.when(q < 4)
        def _():
            a = shift(y, q + 1)
            lax.fori_loop(2 * a, 2 * a + 2, turn, 0)
            part_copy(0, a).start()
            part_copy(1, a).start()

        @pl.when(q > 0)
        def _():
            p = q - 1
            a = shift(y, p + 1)
            part_copy(0, a).wait()
            part_copy(1, a).wait()
            for own_ref, got_ref in ((mine0, core0), (mine1, core1)):
                for b in range(4):
                    own_ref[a, b] = (own_ref[a, b].astype(F32) + got_ref[a, b].astype(F32)).astype(BF)
            for i in (1, 3, 2):
                first_z(p, i).start()

            @pl.when(p < 3)
            def _():
                first_y(p).start()

        return carry

    lax.fori_loop(0, 5, quarter, 0)
    send_pieces(THIRD)

    def first_landed(p, carry):
        for i in (1, 2, 3):
            first_z(p, i).wait()
        return carry

    lax.fori_loop(0, 4, first_landed, 0)
    for p in range(3):
        first_y(p).wait()
    for b in range(4):
        s2a[b] = total(mine0[y, b], r1a, (b,)).astype(BF)
        s2b[b] = total(mine1[b, z], r1b, (b,)).astype(BF)
    stage = []
    for i in (1, 2, 3):
        stage.append(scatter(0, 1, i, s2a.at[shift(z, i)], r2a.at[i - 1], "z"))
        stage.append(scatter(1, 1, i, s2b.at[shift(y, i)], r2b.at[i - 1], "y"))
    send_pieces(FOURTH)
    for cp in stage:
        cp.wait_recv()
    s3a[...] = total(s2a[z], r2a).astype(BF)
    s3b[...] = total(s2b[y], r2b).astype(BF)
    stage = []
    for i in (1, 2, 3):
        to16 = pl.ds(pl.multiple_of(shift(x, i) * 16, 16), 16)
        stage.append(scatter(0, 2, i, s3a.at[to16], r3a.at[i - 1], "x"))
        stage.append(scatter(1, 2, i, s3b.at[to16], r3b.at[i - 1], "x"))
    send_pieces(len(waiting))
    for cp in stage:
        cp.wait_recv()
    sum_a = total(s3a[rows16, :], r3a)
    sum_b = total(s3b[rows16, :], r3b)
    keep_a = jnp.where(c == 0, sum_a[0:8], sum_a[8:16])
    keep_b = jnp.where(c == 0, sum_b[0:8], sum_b[8:16])
    half_out[:, 0:Q] = jnp.where(c == 0, sum_a[8:16], sum_a[0:8])
    half_out[:, Q : 2 * Q] = jnp.where(c == 0, sum_b[8:16], sum_b[0:8])
    last = remote(half_out, last_in, core_s.at[1], core_r.at[1], other)
    last.start()
    last.wait()
    kept = jnp.concatenate([keep_a, keep_b], axis=1)
    given = last_in[...]
    out[:, 0 : 2 * Q] = jnp.where(c == 0, kept, given).astype(BF)
    out[:, 2 * Q :] = jnp.where(c == 0, given, kept).astype(BF)

    for cp in out_copies:
        cp.wait_send()
    for cp in swaps:
        cp.wait()
    for cp in stores:
        cp.wait()


def moe(swapped, tok, routes, gates, gate_weight, up_weight, down_weight):
    vm = lambda *shape: pltpu.VMEM(shape, BF)
    dma = lambda *shape: pltpu.SemaphoreType.DMA(shape)
    any_spec = pl.BlockSpec(memory_space=pl.ANY)
    vmem_spec = pl.BlockSpec(memory_space=pltpu.VMEM)
    smem_spec = pl.BlockSpec(memory_space=pltpu.SMEM)
    like = lambda a: jax.ShapeDtypeStruct(a.shape, a.dtype)
    return pl.pallas_call(
        moe_kernel,
        out_shape=(
            jax.ShapeDtypeStruct((8, D), BF),
            jax.ShapeDtypeStruct((1, EARLY, 256), BF), like(down_weight),
            jax.ShapeDtypeStruct((1, MOVED, 256), BF),
            jax.ShapeDtypeStruct((1,), jnp.int32),
        ),
        in_specs=[smem_spec] + [vmem_spec] * 3 + [any_spec] * 3,
        out_specs=(vmem_spec, any_spec, any_spec, any_spec, smem_spec),
        scratch_shapes=[
            vm(4, 4, 64, W0), vm(4, 4, 64, Q), vm(4, 4, 64, W0), vm(4, 4, 64, Q),
            vm(D, 256), vm(D, 256), vm(256, D),
            vm(4, 4, 64, Q), vm(4, 4, 64, Q), vm(4, 4, 64, Q), vm(4, 4, 64, Q),
            vm(4, 4, 64, Q), vm(4, 4, 64, Q),
            vm(3, 4, 64, Q), vm(3, 4, 64, Q), vm(4, 64, Q), vm(4, 64, Q),
            vm(3, 64, Q), vm(3, 64, Q), vm(64, Q), vm(64, Q), vm(3, 16, Q), vm(3, 16, Q),
            pltpu.VMEM((8, 2 * Q + EXT), F32), pltpu.VMEM((8, 2 * Q + EXT), F32),
            pltpu.VMEM((8, 2 * Q), F32), pltpu.VMEM((8, 2 * Q), F32),
            dma(3), dma(2, PIECES), dma(2, PIECES), dma(2), dma(2),
            dma(2, 3, 3), dma(2, 3, 3), dma(2, 4), dma(2, 4), dma(2, 4), dma(2, 4),
            dma(2, 3, 3), dma(2, 3, 3),
            dma(2, 3, 4), dma(2, 3, 4), dma(3, 4), dma(3, 4),
        ],
        compiler_params=pltpu.CompilerParams(
            collective_id=0, has_side_effects=True, vmem_limit_bytes=64 * 1024 * 1024
        ),
        cost_estimate=pl.CostEstimate(
            flops=6 * 1024 * D * 256, bytes_accessed=33 * 1024 * 1024, transcendentals=1024 * 256
        ),
        name="moe_and_exchange",
    )(swapped, tok, routes, gates, gate_weight, up_weight, down_weight)


def pick_kernel(swapped, mixed, og, ou, od, rg, rx, rd, out, mg, mu, md, bg, bu, bd, in_sem, out_sem):
    out[...] = mixed[...]
    outs, bufs = (mg, mu, md), (bg, bu, bd)
    flag = swapped[lax.rem(lax.axis_index("expert"), EXPERTS // 2)]

    def own(k, start, rows):
        return (og, ou, od)[k].at[0, pl.ds(start, rows)]

    def received(k, start, rows):
        if k == 0 and start < EARLY:
            return rg.at[0, pl.ds(start, rows)]
        if k < 2:
            return rx.at[0, pl.ds(start if k else D + start - EARLY, rows)]
        return rd.at[0, pl.ds(start, rows)]

    def go(source):
        loads, stores = [], []
        for part in range(PIECES):
            for k, (buf, dst) in enumerate(zip(bufs, outs)):
                rows = dst.shape[1] // PIECES
                at = pl.ds(part * rows, rows)
                loads.append(
                    pltpu.make_async_copy(source(k, part * rows, rows), buf.at[at], in_sem.at[k, part])
                )
                stores.append(pltpu.make_async_copy(buf.at[at], dst.at[0, at], out_sem.at[k, part]))
        for cp in loads:
            cp.start()
        for load, store in zip(loads, stores):
            load.wait()
            store.start()
        for cp in stores:
            cp.wait()

    @pl.when(flag == 1)
    def _():
        go(received)

    @pl.when(flag != 1)
    def _():
        go(own)


def pick(swapped, mixed, own, received):
    any_spec = pl.BlockSpec(memory_space=pl.ANY)
    vmem_spec = pl.BlockSpec(memory_space=pltpu.VMEM)
    return pl.pallas_call(
        pick_kernel,
        out_shape=tuple(jax.ShapeDtypeStruct(a.shape, a.dtype) for a in (mixed, *own)),
        in_specs=[pl.BlockSpec(memory_space=pltpu.SMEM), vmem_spec] + [any_spec] * 6,
        out_specs=(vmem_spec,) + (any_spec,) * 3,
        scratch_shapes=[pltpu.VMEM(a.shape[1:], a.dtype) for a in own]
        + [pltpu.SemaphoreType.DMA((3, PIECES)), pltpu.SemaphoreType.DMA((3, PIECES))],
        compiler_params=pltpu.CompilerParams(vmem_limit_bytes=64 * 1024 * 1024),
        name="pick_slab",
    )(swapped, mixed, *own, *received)


def on_device(tokens, routes, gates, swapped, gate_weight, up_weight, down_weight):
    mixed, got_gate, got_down, rest, number = moe(
        swapped, tokens, routes, gates, gate_weight, up_weight, down_weight
    )
    got_rest = lax.switch(number[0], [functools.partial(exchange, p) for p in SETS], rest)
    return pick(
        swapped, mixed, (gate_weight, up_weight, down_weight), (got_gate, got_rest, got_down)
    )


def solution(mesh):
    in_specs = (
        P(("expert", "dp"), None),
        P(("expert", "dp"), None),
        P(("expert", "dp"), None),
        P(),
        P("expert", None, "dp"),
        P("expert", None, "dp"),
        P("expert", "dp", None),
    )
    out_specs = (
        P(("expert", "dp"), None),
        P("expert", None, "dp"),
        P("expert", None, "dp"),
        P("expert", "dp", None),
    )
    return jax.shard_map(
        on_device, mesh=mesh, in_specs=in_specs, out_specs=out_specs, check_vma=False
    )
```
